128 devices in a mesh: seq: 16 (over x, z), mp: 8 (over y, core).
Axes of the slice: x: 4, y: 4, z: 4, core: 2. Of those that a mesh axis runs over, the one named last changes fastest.
Arguments:
- tokens: bfloat16 [12288, 2560], P('seq', 'mp'), may hold values from -6 to 24
- norm_gain: float32 [2560], replicated, may hold values from 0.1 to 1.9
- w_query: bfloat16 [2560, 2048], P(None, 'mp'), may hold values from -0.25 to 0.25
- w_key: bfloat16 [2560, 2048], P(None, 'mp'), may hold values from -0.25 to 0.25
- w_value: bfloat16 [2560, 2048], P(None, 'mp'), may hold values from -0.125 to 0.125
- w_out: bfloat16 [2048, 2560], P('mp'), may hold values from -0.125 to 0.125
- w_up: bfloat16 [6, 2560, 1024], P(None, None, 'mp'), may hold values from -0.125 to 0.125
- w_class: bfloat16 [1024, 14], P('mp'), may hold values from -1 to 1
- starts: int32 [12288], P('seq'), may hold values from 0 to 63487, as said below
- lengths: int32 [12288], P('seq'), may hold values from 1 to 6, as said below
- labels: int32 [63488, 14], P('seq'), may hold values 0 or 1
Outputs:
- features: bfloat16 [63488, 1024], P('seq', 'mp')
- loss: float32 [63488], P('seq')
The draws below stay inside these ranges and needn't reach their ends.
Inputs may be any that keep to these rules, and one draw needn't show every extreme that they name: starts are the running sums of lengths before each token, starting at 0. The tokens of seq index s cover positions from 3968 * s - 5 * d to 3968 * (s + 1) - 5 * e, where d is the value for index s - 1 and e the one for s, each 0 to 128; e is 0 for the last index and reaches 128 on some index. `lengths`: each length is 1 or 6; they sum to 63488; one seq index holds 0 to 256 tokens of length 1.
All inputs are finite; a program needn't handle non-finite values. No bound on the sum of `labels` on one device may be relied on, other than what follows from the above.
Results may differ from the reference program's by a relative error of at most 0.019.
Values may be sent and summed in bfloat16 or wider, within the bound.
A program may use at most 128 MiB of HBM per device.

```python
import math
import jax
import jax.numpy as jnp
from jax import lax

D = 2560
HEADS = 16
HD = 128
C = 1024
CLASSES = 14
KMER = 6
TOK_DEV = 768
N_DEV = 128
TOKENS = 12288
NUCS = 63488


def token_layout(key):
    devices = TOKENS // TOK_DEV
    key_excess, key_where, key_order = jax.random.split(key, 3)
    excess = jax.random.randint(key_excess, (devices,), 0, N_DEV + 1)
    chosen = jax.random.randint(key_where, (), 0, devices - 1)
    places = jnp.arange(devices)
    excess = jnp.where(places == chosen, N_DEV, excess)
    excess = jnp.where(places == devices - 1, 0, excess)
    before = jnp.concatenate([jnp.zeros((1,), jnp.int32), excess[:-1].astype(jnp.int32)])
    single_count = N_DEV + excess.astype(jnp.int32) - before
    orders = jax.vmap(lambda sub_key: jax.random.permutation(sub_key, TOK_DEV))(jax.random.split(key_order, devices))
    single = orders < single_count[:, None]
    lengths = jnp.where(single, 1, KMER).astype(jnp.int32).reshape(-1)
    starts = (jnp.cumsum(lengths) - lengths).astype(jnp.int32)
    return (starts, lengths)


def draw_starts(key, part):
    starts, lengths = token_layout(key)
    return starts


def draw_lengths(key, part):
    starts, lengths = token_layout(key)
    return lengths


def draw_tokens(key, part):
    key = jax.random.fold_in(key, 5)
    values = jax.random.truncated_normal(key, -6.0, 6.0, (TOKENS, D), jnp.float32)
    return values.astype(jnp.bfloat16)


def draw_w_query(key, part):
    key = jax.random.fold_in(key, 13)
    spread = (D // 4) ** (-0.5)
    matrix = jnp.clip(spread * jax.random.normal(key, (D, HEADS * HD), jnp.float32), -0.25, 0.25)
    return matrix.astype(jnp.bfloat16)


def draw_w_key(key, part):
    key = jax.random.fold_in(key, 17)
    spread = (D // 4) ** (-0.5)
    matrix = jnp.clip(spread * jax.random.normal(key, (D, HEADS * HD), jnp.float32), -0.25, 0.25)
    return matrix.astype(jnp.bfloat16)


def plant(drawn, own_key, least, high):
    spot = [jax.random.randint(jax.random.fold_in(own_key, axis), (), 0, length) for axis, length in enumerate(drawn.shape)]
    longest = drawn.shape.index(max(drawn.shape))
    neighbour = spot[:longest] + [(spot[longest] + 1) % drawn.shape[longest]] + spot[longest + 1:]
    return drawn.at[tuple(spot)].set(least).at[tuple(neighbour)].set(high)


def shard_levels(own_key, shape, cuts, low, high):
    gain = 1.0
    for dim, blocks in cuts:
        steps = jax.random.uniform(jax.random.fold_in(jax.random.fold_in(own_key, 6), dim), (blocks,), jnp.float32, low / len(cuts), high / len(cuts))
        gain = gain * jnp.repeat(jnp.exp(steps), shape[dim] // blocks).reshape((-1,) + (1,) * (len(shape) - 1 - dim))
    return gain


def gaussian(stream_key, extent, width, reach, cuts=(), kind=jnp.bfloat16):
    array = width * jax.random.normal(stream_key, extent, jnp.float32)
    if cuts:
        array = array * shard_levels(stream_key, extent, cuts, -0.22, 0.18)
    return jnp.clip(array, -reach, reach).astype(kind)


def setup_inputs(seed: int = 0) -> dict:
    key_of = jax.random.split(jax.random.key(seed), 12)
    return {
        "tokens": draw_tokens(jax.random.fold_in(key_of[11], 71), 0),
        "norm_gain": jnp.clip(1.0 + 0.18 * jax.random.normal(key_of[1], (D,), jnp.float32), 0.1, 1.9),
        "w_query": draw_w_query(jax.random.fold_in(key_of[11], 71), 0),
        "w_key": draw_w_key(jax.random.fold_in(key_of[11], 71), 0),
        "w_value": gaussian(key_of[4], (D, HEADS * HD), D ** -0.5, 0.125, ((1, 8),)),
        "w_out": gaussian(key_of[5], (HEADS * HD, D), (HEADS * HD) ** -0.5, 0.125, ((0, 8),)),
        "w_up": gaussian(key_of[6], (KMER, D, C), D ** -0.5, 0.125, ((2, 8),)),
        "w_class": gaussian(key_of[7], (C, CLASSES), (C // 25) ** -0.5, 1.0, ((0, 8),)),
        "starts": draw_starts(jax.random.fold_in(key_of[11], 71), 0),
        "lengths": draw_lengths(jax.random.fold_in(key_of[11], 71), 0),
        "labels": plant((jax.random.randint(key_of[10], (NUCS, CLASSES), 0, 4) < 1).astype(jnp.int32), jax.random.fold_in(key_of[10], 1), 0, 1),
    }


def layer_norm(values, norm_gain):
    wide = values.astype(jnp.float32)
    row_mean = lax.optimization_barrier(jnp.mean(wide, axis=-1, keepdims=True))
    centred = wide - row_mean
    variance = lax.optimization_barrier(jnp.mean(centred * centred, axis=-1, keepdims=True))
    return (centred * lax.rsqrt(variance + 1e-05) * norm_gain.astype(jnp.float32)).astype(jnp.bfloat16)

def reference(tokens, norm_gain, w_query, w_key, w_value, w_out, w_up, w_class, starts, lengths, labels):
    normed = layer_norm(tokens, norm_gain)
    queries = jnp.dot(normed, w_query, preferred_element_type=jnp.float32).astype(jnp.bfloat16)
    keys = jnp.dot(normed, w_key, preferred_element_type=jnp.float32).astype(jnp.bfloat16)
    values = jnp.dot(normed, w_value, preferred_element_type=jnp.float32).astype(jnp.bfloat16)
    scale = 1.0 / math.sqrt(HD)
    key_heads = keys.reshape(TOKENS, HEADS, HD).transpose(1, 0, 2)
    value_heads = values.reshape(TOKENS, HEADS, HD).transpose(1, 0, 2)
    query_blocks = queries.reshape(TOKENS // TOK_DEV, TOK_DEV, HEADS, HD)

    def one_block(query_block):

        def one_head(inputs):
            query_head, key_head, value_head = inputs
            scores = jnp.dot(query_head, key_head.T, preferred_element_type=jnp.float32) * scale
            highest = lax.optimization_barrier(jnp.max(scores, axis=-1, keepdims=True))
            expos = jnp.exp(scores - highest)
            total = lax.optimization_barrier(jnp.sum(expos, axis=-1, keepdims=True))
            weighted = jnp.dot(expos.astype(jnp.bfloat16), value_head, preferred_element_type=jnp.float32)
            return (weighted / total).astype(jnp.bfloat16)
        return lax.map(one_head, (query_block.transpose(1, 0, 2), key_heads, value_heads))
    attended = lax.map(one_block, query_blocks)
    attended = attended.transpose(0, 2, 1, 3).reshape(TOKENS, HEADS * HD)
    projected = jnp.dot(attended, w_out, preferred_element_type=jnp.float32)
    stream = (tokens.astype(jnp.float32) + projected).astype(jnp.bfloat16)
    expanded = jnp.stack([jax.nn.gelu(jnp.dot(stream, w_up[offset], preferred_element_type=jnp.float32)).astype(jnp.bfloat16) for offset in range(KMER)], axis=1)
    offsets = jnp.arange(KMER, dtype=jnp.int32)
    positions = starts[:, None] + offsets[None, :]
    live = offsets[None, :] < lengths[:, None]
    target = jnp.where(live, positions, NUCS).reshape(-1).astype(jnp.int32)
    features = jnp.zeros((NUCS, C), jnp.bfloat16).at[target].set(expanded.reshape(-1, C), mode='drop')
    logits = jnp.dot(features, w_class, preferred_element_type=jnp.float32)
    picked = lax.optimization_barrier(jnp.sum(labels.astype(jnp.float32) * logits, axis=-1))
    return (features, lax.optimization_barrier(jnp.sum(jax.nn.softplus(logits), axis=-1)) - picked)
```

```python
import functools
import math

import jax
import jax.numpy as jnp
from jax import lax
from jax.experimental import pallas as pl
from jax.experimental.pallas import tpu as pltpu
from jax.sharding import PartitionSpec as P

HD = 128
KMER = 6
TOK = 768
D = 2560
NUC = 3968
LEAD = 640
PIECE = 512
PARTS = 8
CLASSES = 14
MESH = pl.DeviceIdType.MESH
ANY = pl.BlockSpec(memory_space=pl.ANY)
VMEM = pl.BlockSpec(memory_space=pltpu.VMEM)
SMEM = pl.BlockSpec(memory_space=pltpu.SMEM)
BF16 = jnp.bfloat16
F32 = jnp.float32
NT = (((1,), (1,)), ((), ()))


def coords():
    seq = lax.axis_index("seq")
    mp = lax.axis_index("mp")
    return seq // 4, mp // 2, seq % 4, mp % 2


def device(x, y, z, core):
    return {"seq": x * 4 + z, "mp": y * 2 + core}


def greet(partners):
    barrier = pltpu.get_barrier_semaphore()
    for partner in partners:
        pl.semaphore_signal(barrier, inc=1, device_id=partner, device_id_type=MESH)
    pl.semaphore_wait(barrier, len(partners))


def remote(src, dst, send_sem, recv_sem, target):
    return pltpu.make_async_remote_copy(
        src_ref=src, dst_ref=dst, send_sem=send_sem, recv_sem=recv_sem, device_id=target, device_id_type=MESH
    )


class Gather:
    def __init__(self, src, buf, rows, chunks, y_send, y_recv, f_send, f_recv, c_send, c_recv):
        self.src, self.buf, self.step = src, buf, rows // chunks
        self.chunks = chunks
        self.sems = (y_send, y_recv, f_send, f_recv, c_send, c_recv)
        x, y, z, core = coords()
        up, down, far = (y + 1) % 4, (y + 3) % 4, (y + 2) % 4
        self.up, self.down = device(x, up, z, core), device(x, down, z, core)
        self.sibling = device(x, y, z, 1 - core)
        self.own = y * 2 + core
        self.slots = [y * 2 + core, down * 2 + core, up * 2 + core, far * 2 + core]
        self.twins = [y * 2 + 1 - core, down * 2 + 1 - core, up * 2 + 1 - core, far * 2 + 1 - core]

    def partners(self):
        return [self.up, self.down, self.sibling]

    def rows(self, r, part=None):
        if part is None:
            return pl.ds(r * self.step, self.step)
        half = self.step // 2
        return pl.ds(r * self.step + part * half, half)

    def around(self, way, r):
        y_send, y_recv = self.sems[:2]
        rows = self.rows(r)
        return remote(
            self.src.at[rows], self.buf.at[self.own, rows], y_send.at[way, r], y_recv.at[way, r],
            self.up if way == 0 else self.down,
        )

    def arrived(self, way, r):
        y_send, y_recv = self.sems[:2]
        rows = self.rows(r)
        slot = self.buf.at[self.slots[1 + way], rows]
        return remote(slot, slot, y_send.at[way, r], y_recv.at[way, r], self.up if way == 0 else self.down)

    def onward(self, way, r):
        f_send, f_recv = self.sems[2:4]
        slot = self.buf.at[self.slots[1 + way], self.rows(r, way)]
        return remote(slot, slot, f_send.at[way, r], f_recv.at[way, r], self.up if way == 0 else self.down)

    def far_arrived(self, way, r):
        f_send, f_recv = self.sems[2:4]
        slot = self.buf.at[self.slots[3], self.rows(r, way)]
        return remote(slot, slot, f_send.at[way, r], f_recv.at[way, r], self.up if way == 0 else self.down)

    def across(self, which, r, arriving=False):
        c_send, c_recv = self.sems[4:]
        part = which - 3 if which >= 3 else None
        rows = self.rows(r, part)
        slots = self.twins if arriving else self.slots
        slot = self.buf.at[slots[min(which, 3)], rows]
        src = self.src.at[rows] if which == 0 and not arriving else slot
        return remote(src, slot, c_send.at[which, r], c_recv.at[which, r], self.sibling)

    def start(self):
        for r in range(self.chunks):
            self.around(0, r).start()
            self.around(1, r).start()
            self.across(0, r).start()

    def forward(self, r):
        for way in range(2):
            self.arrived(way, r).wait_recv()
            self.onward(way, r).start()
            self.across(1 + way, r).start()

    def forward_far(self, r):
        for way in range(2):
            self.far_arrived(way, r).wait_recv()
            self.across(3 + way, r).start()

    def complete(self, r):
        for which in range(5):
            self.across(which, r, arriving=True).wait_recv()

    def sent(self):
        for r in range(self.chunks):
            for way in range(2):
                self.around(way, r).wait_send()
                self.onward(way, r).wait_send()
            for which in range(5):
                self.across(which, r).wait_send()


def gather_sems(chunks):
    dma = pltpu.SemaphoreType.DMA
    return [dma((2, chunks)), dma((2, chunks)), dma((2, chunks)), dma((2, chunks)), dma((5, chunks)), dma((5, chunks))]


def qkv_kernel(
    tokens, gain, w_query, w_key, w_value, tok_full, q_out, k_out, v_out,
    blocks, weights, rows_v, local, *sems,
):
    chunks = 3
    step = TOK // chunks
    ring = Gather(tokens, blocks, TOK, chunks, *sems)
    own = pltpu.make_async_copy(tokens, blocks.at[ring.own], local.at[0])
    own.start()
    loads = [
        pltpu.make_async_copy(w, weights.at[:, pl.ds(i * 256, 256)], local.at[1 + i])
        for i, w in enumerate((w_query, w_key, w_value))
    ]
    for load in loads:
        load.start()
    greet(ring.partners())
    ring.start()
    own.wait()
    scale = math.log2(math.e) / math.sqrt(HD)
    stores = []
    for r in range(chunks + 1):
        if r < chunks:
            ring.forward(r)
        if r == 0:
            for load in loads:
                load.wait()
            continue
        done = r - 1
        ring.forward_far(done)
        ring.complete(done)
        rows = pl.ds(done * step, step)
        for j in range(PARTS):
            rows_v[rows, pl.ds(j * 320, 320)] = blocks[j, rows, :]
        store = pltpu.make_async_copy(rows_v.at[rows], tok_full.at[rows], local.at[4 + done])
        store.start()
        stores.append(store)
        wide = rows_v[rows, :].astype(F32)
        centred = wide - jnp.mean(wide, axis=-1, keepdims=True)
        variance = jnp.mean(centred * centred, axis=-1, keepdims=True)
        normed = (centred * lax.rsqrt(variance + 1e-05) * gain[...]).astype(BF16)
        qkv = jnp.dot(normed, weights[...], preferred_element_type=F32)
        q_out[:, rows] = (qkv[:, :256] * scale).T.astype(BF16)
        for h in range(2):
            k_out[h, rows, :] = qkv[:, 256 + h * HD : 256 + (h + 1) * HD].astype(BF16)
        v_out[:, rows] = qkv[:, 512:].T.astype(BF16)
    ring.sent()
    for store in stores:
        store.wait()


def project(tokens, gain, w_query, w_key, w_value):
    return pl.pallas_call(
        qkv_kernel,
        out_shape=(
            jax.ShapeDtypeStruct((TOK, D), BF16),
            jax.ShapeDtypeStruct((256, TOK), BF16),
            jax.ShapeDtypeStruct((2, TOK, HD), BF16),
            jax.ShapeDtypeStruct((256, TOK), BF16),
        ),
        in_specs=[ANY, VMEM, ANY, ANY, ANY],
        out_specs=(ANY, VMEM, VMEM, VMEM),
        scratch_shapes=[
            pltpu.VMEM((PARTS, TOK, 320), BF16),
            pltpu.VMEM((D, 768), BF16),
            pltpu.VMEM((TOK, D), BF16),
            pltpu.SemaphoreType.DMA((7,)),
            *gather_sems(3),
        ],
        compiler_params=pltpu.CompilerParams(
            collective_id=0, has_side_effects=True, vmem_limit_bytes=56 << 20
        ),
    )(tokens, gain, w_query, w_key, w_value)


def pick(index, options):
    value = options[-1]
    for i in range(len(options) - 2, -1, -1):
        value = jnp.where(index == i, options[i], value)
    return value


UNITS = [
    (0, 0), (1, 0), (2, 0), (0, 1), (1, 1), (2, 1), (0, 2), (1, 2), (2, 2),
    (3, 0), (3, 1), (3, 2), (3, 3), (1, 3), (2, 3), (0, 3),
]


def attend_kernel(
    q_in, k_in, v_in, w_out, att, w_full,
    qb, kb, vb, acc, top, o_send, l_send, o_recv, l_recv,
    local, q_ss, q_rs, k_ss, k_rs, v_ss, v_rs, o_ss, o_rs, l_ss, l_rs, *sems,
):
    x, y, z, core = coords()
    ring = Gather(w_out, w_full, 256, 2, *sems)

    def along(axis, by):
        if axis == 0:
            return device((x + by + 4) % 4, y, z, core)
        return device(x, y, (z + by + 4) % 4, core)

    offsets = {1: 1, 2: -1, 3: 2}

    def move(kind, h, slot):
        axis = 1 - h if kind == "q" else h
        target = along(axis, -offsets[slot])
        if kind == "q":
            src, dst, ss, rs = q_in.at[pl.ds(h * HD, HD)], qb.at[h, slot], q_ss, q_rs
        elif kind == "k":
            src, dst, ss, rs = k_in.at[h], kb.at[h, slot], k_ss, k_rs
        else:
            src, dst, ss, rs = v_in.at[pl.ds(h * HD, HD)], vb.at[h, slot], v_ss, v_rs
        return remote(src, dst, ss.at[h, slot], rs.at[h, slot], target)

    own = []
    for h in range(2):
        own.append(pltpu.make_async_copy(q_in.at[pl.ds(h * HD, HD)], qb.at[h, 0], local.at[0, h]))
        own.append(pltpu.make_async_copy(k_in.at[h], kb.at[h, 0], local.at[1, h]))
        own.append(pltpu.make_async_copy(v_in.at[pl.ds(h * HD, HD)], vb.at[h, 0], local.at[2, h]))
    own_w = pltpu.make_async_copy(w_out, w_full.at[ring.own], local.at[3, 0])
    for copy in own:
        copy.start()
    own_w.start()
    greet([along(a, by) for a in range(2) for by in (1, -1, 2)] + ring.partners())
    for kinds, slots in (("q", (1, 2)), ("kv", (1, 2)), ("q", (3,)), ("kv", (3,))):
        for slot in slots:
            for kind in kinds:
                for h in range(2):
                    move(kind, h, slot).start()
    ring.start()
    top[...] = jnp.full(top.shape, -1e30, F32)
    acc[...] = jnp.zeros(acc.shape, F32)
    for copy in own:
        copy.wait()

    ones = jnp.ones((16, TOK), BF16)

    def partial(h, a):
        total = acc[h, a, HD : HD + 8, :]
        return acc[h, a, :HD, :] / total[:1], top[h, a] + jnp.log2(total)

    def give(h, slot):
        by = pick(slot - 1, [1, -1, 2])
        target = along(1 - h, by)
        return [
            remote(o_send.at[h, slot - 1], o_recv.at[h, slot - 1], o_ss.at[h, slot - 1], o_rs.at[h, slot - 1], target),
            remote(l_send.at[h, slot - 1], l_recv.at[h, slot - 1], l_ss.at[h, slot - 1], l_rs.at[h, slot - 1], target),
        ]

    def unit(i, carry):
        def arrivals(kinds, slot):
            for kind in kinds:
                for h in range(2):
                    move(kind, h, slot).wait_recv()

        for index, kinds, slot in ((1, "q", 1), (2, "q", 2), (3, "kv", 1), (6, "kv", 2), (9, "q", 3), (12, "kv", 3)):
            pl.when(i == index)(functools.partial(arrivals, kinds, slot))
        pl.when(i == 7)(functools.partial(ring.forward, 0))
        pl.when(i == 13)(functools.partial(ring.forward, 1))
        a = pick(i, [u[0] for u in UNITS])
        b = pick(i, [u[1] for u in UNITS])
        scores = [
            jnp.dot(kb[h, b], qb[h, a], preferred_element_type=F32) for h in range(2)
        ]
        for h in range(2):
            s = scores[h]
            before = top[h, a]
            now = jnp.maximum(before, jnp.max(s, axis=0, keepdims=True))
            weights = jnp.exp2(s - now[:1]).astype(BF16)
            factor = jnp.exp2(before - now)
            lhs = jnp.concatenate([vb[h, b], ones], axis=0)
            added = jnp.dot(lhs, weights, preferred_element_type=F32)
            acc[h, a] = acc[h, a] * factor[:1] + added
            top[h, a] = now

        @pl.when(jnp.logical_and(i >= 12, i < 15))
        def _():
            for h in range(2):
                value, level = partial(h, a)
                o_send[h, a - 1] = value.astype(BF16)
                l_send[h, a - 1] = level
                for copy in give(h, a):
                    copy.start()

        return carry

    lax.fori_loop(0, len(UNITS), unit, 0)
    for r in range(2):
        ring.forward_far(r)
    for h in range(2):
        value, level = partial(h, 0)
        for slot in range(1, 4):
            for copy in give(h, slot):
                copy.wait_recv()
        levels = [level] + [l_recv[h, i] for i in range(3)]
        highest = functools.reduce(jnp.maximum, levels)
        shares = [jnp.exp2(one - highest) for one in levels]
        total = functools.reduce(jnp.add, shares)
        shares = [share / total for share in shares]
        value = value * shares[0][:1]
        for i in range(3):
            value = value + o_recv[h, i].astype(F32) * shares[1 + i][:1]
        att[:, pl.ds(h * HD, HD)] = value.T.astype(BF16)
    own_w.wait()
    for r in range(2):
        ring.complete(r)
    ring.sent()
    for h in range(2):
        for slot in range(1, 4):
            for kind in "qkv":
                move(kind, h, slot).wait_send()
            for copy in give(h, slot):
                copy.wait_send()


def attend(q, k, v, w_out):
    dma = pltpu.SemaphoreType.DMA
    return pl.pallas_call(
        attend_kernel,
        out_shape=(
            jax.ShapeDtypeStruct((TOK, 256), BF16),
            jax.ShapeDtypeStruct((PARTS, 256, D), BF16),
        ),
        in_specs=[ANY] * 4,
        out_specs=(VMEM, ANY),
        scratch_shapes=[
            pltpu.VMEM((2, 4, HD, TOK), BF16),
            pltpu.VMEM((2, 4, TOK, HD), BF16),
            pltpu.VMEM((2, 4, HD, TOK), BF16),
            pltpu.VMEM((2, 4, HD + 16, TOK), F32),
            pltpu.VMEM((2, 4, 8, TOK), F32),
            pltpu.VMEM((2, 3, HD, TOK), BF16),
            pltpu.VMEM((2, 3, 8, TOK), F32),
            pltpu.VMEM((2, 3, HD, TOK), BF16),
            pltpu.VMEM((2, 3, 8, TOK), F32),
            dma((4, 2)),
            *[dma((2, 4)) for _ in range(6)],
            *[dma((2, 3)) for _ in range(4)],
            *gather_sems(2),
        ],
        compiler_params=pltpu.CompilerParams(
            collective_id=1, has_side_effects=True, vmem_limit_bytes=56 << 20
        ),
    )(q, k, v, w_out)


def gelu(x):
    return 0.5 * x * (1.0 + jnp.tanh(math.sqrt(2.0 / math.pi) * (x + 0.044715 * x * x * x)))


def expand_kernel(att, tok, w_full, w_up, out, blocks, wo_v, wu_v, tok_v, local, *sems):
    chunks = 3
    step = TOK // chunks
    ring = Gather(att, blocks, TOK, chunks, *sems)
    loads = [pltpu.make_async_copy(att, blocks.at[ring.own], local.at[0])]
    loads += [pltpu.make_async_copy(tok, tok_v, local.at[1])]
    loads += [
        pltpu.make_async_copy(w_up.at[j], wu_v.at[:, pl.ds(j * HD, HD)], local.at[2 + j]) for j in range(KMER)
    ]
    loads += [
        pltpu.make_async_copy(w_full.at[j], wo_v.at[pl.ds(j * 256, 256)], local.at[8 + j]) for j in range(PARTS)
    ]
    for load in loads:
        load.start()
    greet(ring.partners())
    ring.start()
    for r in range(chunks + 1):
        if r < chunks:
            ring.forward(r)
        if r == 0:
            for load in loads:
                load.wait()
            continue
        done = r - 1
        ring.forward_far(done)
        ring.complete(done)
        rows = pl.ds(done * step, step)
        joined = jnp.concatenate([blocks[j, rows, :] for j in range(PARTS)], axis=1)
        projected = jnp.dot(joined, wo_v[...], preferred_element_type=F32)
        stream = (tok_v[rows, :].astype(F32) + projected).astype(BF16)
        raised = jnp.dot(stream, wu_v[...], preferred_element_type=F32)
        out[rows, :] = gelu(raised).astype(BF16)
    ring.sent()


def expand(att, tok, w_full, w_up):
    return pl.pallas_call(
        expand_kernel,
        out_shape=jax.ShapeDtypeStruct((TOK, KMER * HD), BF16),
        in_specs=[ANY] * 4,
        out_specs=VMEM,
        scratch_shapes=[
            pltpu.VMEM((PARTS, TOK, 256), BF16),
            pltpu.VMEM((PARTS * 256, D), BF16),
            pltpu.VMEM((D, KMER * HD), BF16),
            pltpu.VMEM((TOK, D), BF16),
            pltpu.SemaphoreType.DMA((16,)),
            *gather_sems(3),
        ],
        compiler_params=pltpu.CompilerParams(
            collective_id=2, has_side_effects=True, vmem_limit_bytes=56 << 20
        ),
    )(att, tok, w_full, w_up)


def place_kernel(starts, lengths, expanded, w_class, own, lead, logits, wide, placed):
    for j in range(KMER):
        wide[pl.ds(j, TOK, stride=8), :] = expanded[:, j * HD : (j + 1) * HD].astype(F32)
    placed[:LEAD, :] = jnp.zeros((LEAD, HD), F32)
    placed[NUC:, :] = jnp.zeros((LEAD + 16, HD), F32)
    shift = LEAD - lax.axis_index("seq") * NUC

    def one(t, carry):
        placed[pl.ds(starts[t] + shift, 8), :] = wide[pl.ds(pl.multiple_of(t * 8, 8), 8), :]
        return carry

    lax.fori_loop(0, TOK, one, 0, unroll=8)
    end = starts[TOK - 1] + lengths[TOK - 1] + shift
    placed[pl.ds(end, 8), :] = jnp.zeros((8, HD), F32)
    lead[...] = placed[:LEAD, :].astype(BF16)
    rows = placed[LEAD : LEAD + NUC, :].astype(BF16)
    own[...] = rows
    logits[:, :NUC] = lax.dot_general(w_class[...], rows, NT, preferred_element_type=F32)
    logits[:, NUC:] = jnp.zeros((16, PARTS * PIECE - NUC), F32)


def place(starts, lengths, expanded, w_class):
    return pl.pallas_call(
        place_kernel,
        out_shape=(
            jax.ShapeDtypeStruct((NUC, HD), BF16),
            jax.ShapeDtypeStruct((LEAD, HD), BF16),
            jax.ShapeDtypeStruct((16, PARTS * PIECE), F32),
        ),
        in_specs=[SMEM, SMEM, VMEM, VMEM],
        out_specs=(VMEM, VMEM, VMEM),
        scratch_shapes=[
            pltpu.VMEM((TOK * 8, HD), F32),
            pltpu.VMEM((LEAD + NUC + 16, HD), F32),
        ],
        compiler_params=pltpu.CompilerParams(vmem_limit_bytes=48 << 20),
    )(starts, lengths, expanded, w_class)


def loss_kernel(
    lead, logits, w_class, labels, arriving, loss,
    pieces, received, lab, mine, lead_ss, lead_rs, p_ss, p_rs, a_ss, a_rs, lab_sem,
):
    seq = lax.axis_index("seq")
    mp = lax.axis_index("mp")
    before = {"seq": (seq + 15) % 16, "mp": mp}
    after = {"seq": (seq + 1) % 16, "mp": mp}
    others = [{"seq": seq, "mp": (mp + d) % PARTS} for d in range(1, PARTS)]
    head = 384
    lab_head = pltpu.make_async_copy(
        labels.at[pl.ds(mp * PIECE, head)], lab.at[pl.ds(0, head)], lab_sem.at[0]
    )
    lab_tail = pltpu.make_async_copy(
        labels.at[pl.ds(jnp.minimum(mp, PARTS - 2) * PIECE + head, PIECE - head)],
        lab.at[pl.ds(head, PIECE - head)], lab_sem.at[1],
    )
    lab_head.start()
    lab_tail.start()
    greet([before, after] + others)
    shift = remote(lead, arriving, lead_ss, lead_rs, before)
    shift.start()

    def piece(j):
        return logits[:, j * PIECE : (j + 1) * PIECE].astype(BF16)

    def copies(d):
        return remote(
            pieces.at[(mp + d) % PARTS], received.at[d - 1], p_ss.at[d - 1], p_rs.at[d - 1], others[d - 1]
        )

    for j in range(6):
        pieces[j] = piece(j)
    shift.wait_recv()
    late = NUC - LEAD
    logits[:, late:NUC] = logits[:, late:NUC] + lax.dot_general(
        w_class[...], arriving[...], NT, preferred_element_type=F32
    )
    for j in range(6, PARTS):
        pieces[j] = piece(j)
    for d in range(1, PARTS):
        copies(d).start()
    lab_head.wait()
    lab_tail.wait()
    picked = (
        lax.broadcasted_iota(jnp.int32, (16, CLASSES), 0) == lax.broadcasted_iota(jnp.int32, (16, CLASSES), 1)
    ).astype(BF16)
    marks = lax.dot_general(picked, lab[...].astype(BF16), NT, preferred_element_type=F32)
    for d in range(1, PARTS):
        copies(d).wait_recv()
    total = pieces[mp].astype(F32)
    for d in range(1, PARTS):
        total = total + received[d - 1].astype(F32)
    softplus = jnp.maximum(total, 0.0) + jnp.log(1.0 + jnp.exp(-jnp.abs(total)))
    terms = softplus - marks * total
    real = lax.broadcasted_iota(jnp.int32, terms.shape, 0) < CLASSES
    summed = jnp.sum(jnp.where(real, terms, 0.0), axis=0, keepdims=True)
    mine[...] = jnp.broadcast_to(summed, (8, PIECE))

    def spread(d):
        return remote(mine, loss.at[mp], a_ss.at[d - 1], a_rs.at[d - 1], others[d - 1])

    for d in range(1, PARTS):
        spread(d).start()
    loss[mp] = mine[...]
    for d in range(1, PARTS):
        spread(d).wait_recv()
    shift.wait_send()
    for d in range(1, PARTS):
        copies(d).wait_send()
        spread(d).wait_send()


def losses(lead, logits, w_class, labels):
    dma = pltpu.SemaphoreType.DMA
    return pl.pallas_call(
        loss_kernel,
        out_shape=(
            jax.ShapeDtypeStruct((LEAD, HD), BF16),
            jax.ShapeDtypeStruct((PARTS, 8, PIECE), F32),
        ),
        in_specs=[VMEM, VMEM, VMEM, ANY],
        out_specs=(VMEM, VMEM),
        scratch_shapes=[
            pltpu.VMEM((PARTS, 16, PIECE), BF16),
            pltpu.VMEM((PARTS - 1, 16, PIECE), BF16),
            pltpu.VMEM((PIECE, CLASSES), jnp.int32),
            pltpu.VMEM((8, PIECE), F32),
            dma, dma, dma((7,)), dma((7,)), dma((7,)), dma((7,)), dma((2,)),
        ],
        compiler_params=pltpu.CompilerParams(
            collective_id=3, has_side_effects=True, vmem_limit_bytes=32 << 20
        ),
    )(lead, logits, w_class, labels)


def per_device(
    tokens, norm_gain, w_query, w_key, w_value, w_out, w_up, w_class, starts, lengths, labels
):
    class_rows = jnp.pad(w_class.T, ((0, 2), (0, 0)))
    tok_full, q, k, v = project(tokens, norm_gain.reshape(1, D), w_query, w_key, w_value)
    att, w_full = attend(q, k, v, w_out)
    expanded = expand(att, tok_full, w_full, w_up)
    own, lead, logits = place(starts, lengths, expanded, class_rows)
    arriving, loss = losses(lead, logits, class_rows, labels)
    features = own.at[NUC - LEAD :].add(arriving)
    return (features, loss[:, 0, :].reshape(-1)[:NUC])


def solution(mesh):
    return jax.shard_map(
        per_device,
        mesh=mesh,
        in_specs=(
            P("seq", "mp"),
            P(),
            P(None, "mp"),
            P(None, "mp"),
            P(None, "mp"),
            P("mp", None),
            P(None, None, "mp"),
            P("mp", None),
            P("seq"),
            P("seq"),
            P("seq", None),
        ),
        out_specs=(P("seq", "mp"), P("seq")),
        check_vma=False,
    )
```

```python
import functools
import math

import jax
import jax.numpy as jnp
from jax import lax
from jax.experimental import pallas as pl
from jax.experimental.pallas import tpu as pltpu
from jax.sharding import PartitionSpec as P

HD = 128
KMER = 6
TOK = 768
D = 2560
NUC = 3968
LEAD = 640
PIECE = 512
PARTS = 8
CLASSES = 14
MESH = pl.DeviceIdType.MESH
ANY = pl.BlockSpec(memory_space=pl.ANY)
VMEM = pl.BlockSpec(memory_space=pltpu.VMEM)
SMEM = pl.BlockSpec(memory_space=pltpu.SMEM)
BF16 = jnp.bfloat16
F32 = jnp.float32
NT = (((1,), (1,)), ((), ()))


def coords():
    seq = lax.axis_index("seq")
    mp = lax.axis_index("mp")
    return seq // 4, mp // 2, seq % 4, mp % 2


def device(x, y, z, core):
    return {"seq": x * 4 + z, "mp": y * 2 + core}


def greet(partners):
    barrier = pltpu.get_barrier_semaphore()
    for partner in partners:
        pl.semaphore_signal(barrier, inc=1, device_id=partner, device_id_type=MESH)
    pl.semaphore_wait(barrier, len(partners))


def remote(src, dst, send_sem, recv_sem, target):
    return pltpu.make_async_remote_copy(
        src_ref=src, dst_ref=dst, send_sem=send_sem, recv_sem=recv_sem, device_id=target, device_id_type=MESH
    )


class Gather:
    def __init__(self, src, buf, extent, chunks, y_send, y_recv, f_send, f_recv, c_send, c_recv, wide=0):
        self.src, self.buf, self.step, self.wide = src, buf, extent // chunks, wide
        self.chunks = chunks
        self.sems = (y_send, y_recv, f_send, f_recv, c_send, c_recv)
        x, y, z, core = coords()
        up, down, far = (y + 1) % 4, (y + 3) % 4, (y + 2) % 4
        self.up, self.down = device(x, up, z, core), device(x, down, z, core)
        self.sibling = device(x, y, z, 1 - core)
        self.own = y * 2 + core
        self.slots = [y * 2 + core, down * 2 + core, up * 2 + core, far * 2 + core]
        self.twins = [y * 2 + 1 - core, down * 2 + 1 - core, up * 2 + 1 - core, far * 2 + 1 - core]

    def partners(self):
        return [self.up, self.down, self.sibling]

    def cut(self, r, part):
        if part is None:
            return pl.ds(r * self.step, self.step)
        half = self.step // 2
        return pl.ds(r * self.step + part * half, half)

    def mine(self, r):
        cut = self.cut(r, None)
        return self.src.at[:, cut] if self.wide else self.src.at[cut]

    def at(self, slot, r, part=None):
        cut = self.cut(r, part)
        if self.wide:
            return self.buf.at[pl.ds(pl.multiple_of(slot * self.wide, 16), self.wide), cut]
        return self.buf.at[slot, cut]

    def toward(self, way):
        return self.up if way == 0 else self.down

    def around(self, way, r):
        y_send, y_recv = self.sems[:2]
        return remote(self.mine(r), self.at(self.own, r), y_send.at[way, r], y_recv.at[way, r], self.toward(way))

    def arrived(self, way, r):
        y_send, y_recv = self.sems[:2]
        slot = self.at(self.slots[1 + way], r)
        return remote(slot, slot, y_send.at[way, r], y_recv.at[way, r], self.toward(way))

    def onward(self, way, r):
        f_send, f_recv = self.sems[2:4]
        slot = self.at(self.slots[1 + way], r, way)
        return remote(slot, slot, f_send.at[way, r], f_recv.at[way, r], self.toward(way))

    def far_arrived(self, way, r):
        f_send, f_recv = self.sems[2:4]
        slot = self.at(self.slots[3], r, way)
        return remote(slot, slot, f_send.at[way, r], f_recv.at[way, r], self.toward(way))

    def across(self, which, r, arriving=False):
        c_send, c_recv = self.sems[4:]
        part = which - 3 if which >= 3 else None
        slots = self.twins if arriving else self.slots
        slot = self.at(slots[min(which, 3)], r, part)
        src = self.mine(r) if which == 0 and not arriving else slot
        return remote(src, slot, c_send.at[which, r], c_recv.at[which, r], self.sibling)

    def start(self, first=0, last=None):
        for r in range(first, self.chunks if last is None else last):
            self.around(0, r).start()
            self.around(1, r).start()
            self.across(0, r).start()

    def forward(self, r):
        for way in range(2):
            self.arrived(way, r).wait_recv()
            self.onward(way, r).start()
            self.across(1 + way, r).start()

    def forward_far(self, r):
        for way in range(2):
            self.far_arrived(way, r).wait_recv()
            self.across(3 + way, r).start()

    def complete(self, r):
        for which in range(5):
            self.across(which, r, arriving=True).wait_recv()

    def sent(self):
        for r in range(self.chunks):
            for way in range(2):
                self.around(way, r).wait_send()
                self.onward(way, r).wait_send()
            for which in range(5):
                self.across(which, r).wait_send()


def gather_sems(chunks):
    dma = pltpu.SemaphoreType.DMA
    return [dma((2, chunks)), dma((2, chunks)), dma((2, chunks)), dma((2, chunks)), dma((5, chunks)), dma((5, chunks))]


def pick(index, options):
    value = options[-1]
    for i in range(len(options) - 2, -1, -1):
        value = jnp.where(index == i, options[i], value)
    return value


CHUNKS = 3
STEP = TOK // CHUNKS
PARTS_W = 4
UNITS = [
    (0, 0), (1, 0), (2, 0), (1, 1), (2, 1), (1, 2), (2, 2), (0, 1),
    (3, 0), (3, 1), (3, 2), (3, 3), (1, 3), (2, 3), (0, 2), (0, 3),
]


def attend_kernel(
    tokens, gain, w_query, w_key, w_value, w_out, w_up, att, w_full, base,
    xb, weights, turned, up_in, up_turned, gains, qb, kb, vb, acc, top, o_send, l_send, o_recv, l_recv,
    local, q_ss, q_rs, k_ss, k_rs, v_ss, v_rs, o_ss, o_rs, l_ss, l_rs, *sems,
):
    x, y, z, core = coords()
    tok_ring = Gather(tokens, xb, TOK, CHUNKS, *sems[:6], wide=D // PARTS)
    ring = Gather(w_out, w_full, 256, PARTS_W, *sems[6:])

    def along(axis, by):
        if axis == 0:
            return device((x + by + 4) % 4, y, z, core)
        return device(x, y, (z + by + 4) % 4, core)

    offsets = {1: 1, 2: -1, 3: 2}

    def move(kind, h, slot, r):
        target = along(1 - h if kind == "q" else h, -offsets[slot])
        part = pl.ds(r * STEP, STEP)
        if kind == "q":
            src, dst, ss, rs = qb.at[h, 0, :, part], qb.at[h, slot, :, part], q_ss, q_rs
        elif kind == "k":
            src, dst, ss, rs = kb.at[h, 0, part], kb.at[h, slot, part], k_ss, k_rs
        else:
            src, dst, ss, rs = vb.at[h, 0, :, part], vb.at[h, slot, :, part], v_ss, v_rs
        return remote(src, dst, ss.at[h, slot, r], rs.at[h, slot, r], target)

    def send(slots, r):
        for kind in "qkv":
            for slot in slots:
                for h in range(2):
                    move(kind, h, slot, r).start()

    def lift(r):
        cut = pl.ds(r * STEP, STEP)
        base[cut, :] = jnp.dot(up_turned[...], xb[:, cut], preferred_element_type=F32).T

    own = pltpu.make_async_copy(
        tokens, xb.at[pl.ds(pl.multiple_of(tok_ring.own * (D // PARTS), 16), D // PARTS)], local.at[0]
    )
    own.start()
    loads = [pltpu.make_async_copy(w, weights.at[i], local.at[1 + i]) for i, w in enumerate((w_query, w_key, w_value))]
    for load in loads:
        load.start()
    own_w = pltpu.make_async_copy(w_out, w_full.at[ring.own], local.at[4])
    own_w.start()
    ups = [pltpu.make_async_copy(w_up.at[j], up_in.at[:, pl.ds(j * HD, HD)], local.at[5 + j]) for j in range(KMER)]
    for load in ups:
        load.start()
    greet([along(a, by) for a in range(2) for by in (1, -1, 2)] + ring.partners())
    tok_ring.start(0, 1)
    for i in range(D // HD):
        gains[pl.ds(i * HD, HD), :] = jnp.broadcast_to(gain[pl.ds(i, 1), :], (HD, HD)).T

    def turn(i):
        loads[i].wait()
        for j in range(D // 256):
            turned[pl.ds(i * 256, 256), pl.ds(j * 256, 256)] = weights[i, pl.ds(j * 256, 256), :].T

    def turn_up(i):
        for j in range(D // 256):
            up_turned[pl.ds(i * 256, 256), pl.ds(j * 256, 256)] = up_in[pl.ds(j * 256, 256), pl.ds(i * 256, 256)].T

    scale = math.log2(math.e) / math.sqrt(HD)

    def heads(r):
        tok_ring.complete(r)
        cut = pl.ds(r * STEP, STEP)
        wide = xb[:, cut].astype(F32)
        centred = wide - jnp.mean(wide, axis=0, keepdims=True)
        variance = jnp.mean(centred * centred, axis=0, keepdims=True)
        column = jnp.concatenate([gains[...]] * (STEP // HD), axis=1)
        normed = (centred * lax.rsqrt(variance + 1e-05) * column).astype(BF16)
        qkv = jnp.dot(turned[...], normed, preferred_element_type=F32)
        for h in range(2):
            at = h * HD
            qb[h, 0, :, cut] = (qkv[at : at + HD] * scale).astype(BF16)
            kb[h, 0, cut, :] = qkv[256 + at : 256 + at + HD].T.astype(BF16)
            vb[h, 0, :, cut] = qkv[512 + at : 512 + at + HD].astype(BF16)
        send((1, 2), r)

    turn(0)
    tok_ring.start(1, 2)
    turn(1)
    turn(2)
    own.wait()
    tok_ring.forward(0)
    tok_ring.start(2, 3)
    for load in ups:
        load.wait()
    turn_up(0)
    top[...] = jnp.full(top.shape, -1e30, F32)
    acc[...] = jnp.zeros(acc.shape, F32)
    tok_ring.forward(1)
    tok_ring.forward_far(0)
    turn_up(1)
    heads(0)
    tok_ring.forward(2)
    tok_ring.forward_far(1)
    ring.start()
    heads(1)
    tok_ring.forward_far(2)
    turn_up(2)
    heads(2)

    ones = jnp.ones((16, TOK), BF16)

    def partial(h, a):
        total = acc[h, a, HD : HD + 8, :]
        return acc[h, a, :HD, :] / total[:1], top[h, a] + jnp.log2(total)

    def give(h, slot):
        by = pick(slot - 1, [1, -1, 2])
        target = along(1 - h, by)
        return [
            remote(o_send.at[h, slot - 1], o_recv.at[h, slot - 1], o_ss.at[h, slot - 1], o_rs.at[h, slot - 1], target),
            remote(l_send.at[h, slot - 1], l_recv.at[h, slot - 1], l_ss.at[h, slot - 1], l_rs.at[h, slot - 1], target),
        ]

    def unit(i, carry):
        def arrivals(kinds, slot):
            for kind in kinds:
                for h in range(2):
                    for r in range(CHUNKS):
                        move(kind, h, slot, r).wait_recv()

        @pl.when(i == 1)
        def _():
            for r in range(CHUNKS):
                send((3,), r)
            lift(0)
            lift(1)

        for index, kinds, slot in ((1, "q", 1), (2, "q", 2), (3, "kv", 1), (5, "kv", 2), (8, "q", 3), (11, "kv", 3)):
            pl.when(i == index)(functools.partial(arrivals, kinds, slot))
        for r, index in enumerate((2, 5, 9, 12)):
            pl.when(i == index)(functools.partial(ring.forward, r))
        a = pick(i, [u[0] for u in UNITS])
        b = pick(i, [u[1] for u in UNITS])
        scores = [
            jnp.dot(kb[h, b], qb[h, a], preferred_element_type=F32) for h in range(2)
        ]
        for h in range(2):
            s = scores[h]
            before = top[h, a]
            now = jnp.maximum(before, jnp.max(s, axis=0, keepdims=True))
            weights = jnp.exp2(s - now[:1]).astype(BF16)
            factor = jnp.exp2(before - now)
            lhs = jnp.concatenate([vb[h, b], ones], axis=0)
            added = jnp.dot(lhs, weights, preferred_element_type=F32)
            acc[h, a] = acc[h, a] * factor[:1] + added
            top[h, a] = now

        @pl.when(jnp.logical_and(i >= 11, i < 14))
        def _():
            for h in range(2):
                value, level = partial(h, a)
                o_send[h, a - 1] = value.astype(BF16)
                l_send[h, a - 1] = level
                for copy in give(h, a):
                    copy.start()

        return carry

    lax.fori_loop(0, len(UNITS), unit, 0)
    lift(CHUNKS - 1)
    for r in range(PARTS_W):
        ring.forward_far(r)
    for h in range(2):
        value, level = partial(h, 0)
        for slot in range(1, 4):
            for copy in give(h, slot):
                copy.wait_recv()
        levels = [level] + [l_recv[h, i] for i in range(3)]
        highest = functools.reduce(jnp.maximum, levels)
        shares = [jnp.exp2(one - highest) for one in levels]
        total = functools.reduce(jnp.add, shares)
        shares = [share / total for share in shares]
        value = value * shares[0][:1]
        for i in range(3):
            value = value + o_recv[h, i].astype(F32) * shares[1 + i][:1]
        att[:, pl.ds(h * HD, HD)] = value.T.astype(BF16)
    own_w.wait()
    for r in range(PARTS_W):
        ring.complete(r)
    tok_ring.sent()
    ring.sent()
    for h in range(2):
        for slot in range(1, 4):
            for kind in "qkv":
                for r in range(CHUNKS):
                    move(kind, h, slot, r).wait_send()
            for copy in give(h, slot):
                copy.wait_send()


def attend(tokens, gain, w_query, w_key, w_value, w_out, w_up):
    dma = pltpu.SemaphoreType.DMA
    return pl.pallas_call(
        attend_kernel,
        out_shape=(
            jax.ShapeDtypeStruct((TOK, 256), BF16),
            jax.ShapeDtypeStruct((PARTS, 256, D), BF16),
            jax.ShapeDtypeStruct((TOK, KMER * HD), F32),
        ),
        in_specs=[ANY, VMEM, ANY, ANY, ANY, ANY, ANY],
        out_specs=(VMEM, ANY, VMEM),
        scratch_shapes=[
            pltpu.VMEM((D, TOK), BF16),
            pltpu.VMEM((3, D, 256), BF16),
            pltpu.VMEM((768, D), BF16),
            pltpu.VMEM((D, KMER * HD), BF16),
            pltpu.VMEM((KMER * HD, D), BF16),
            pltpu.VMEM((D, HD), F32),
            pltpu.VMEM((2, 4, HD, TOK), BF16),
            pltpu.VMEM((2, 4, TOK, HD), BF16),
            pltpu.VMEM((2, 4, HD, TOK), BF16),
            pltpu.VMEM((2, 4, HD + 16, TOK), F32),
            pltpu.VMEM((2, 4, 8, TOK), F32),
            pltpu.VMEM((2, 3, HD, TOK), BF16),
            pltpu.VMEM((2, 3, 8, TOK), F32),
            pltpu.VMEM((2, 3, HD, TOK), BF16),
            pltpu.VMEM((2, 3, 8, TOK), F32),
            dma((5 + KMER,)),
            *[dma((2, 4, CHUNKS)) for _ in range(6)],
            *[dma((2, 3)) for _ in range(4)],
            *gather_sems(CHUNKS),
            *gather_sems(PARTS_W),
        ],
        compiler_params=pltpu.CompilerParams(
            collective_id=0, has_side_effects=True, vmem_limit_bytes=56 << 20
        ),
    )(tokens, gain, w_query, w_key, w_value, w_out, w_up)


def gelu(x):
    return 0.5 * x * (1.0 + jnp.tanh(math.sqrt(2.0 / math.pi) * (x + 0.044715 * x * x * x)))


def expand_kernel(att, base, w_full, w_up, out, blocks, wo_v, wu_v, base_v, joint, local, *sems):
    ring = Gather(att, blocks, TOK, CHUNKS, *sems)
    ups = [pltpu.make_async_copy(w_up.at[j], wu_v.at[:, pl.ds(j * HD, HD)], local.at[2 + j]) for j in range(KMER)]
    outs = [pltpu.make_async_copy(w_full.at[j], wo_v.at[j], local.at[8 + j]) for j in range(PARTS)]
    lifted = pltpu.make_async_copy(base, base_v, local.at[1])
    own = pltpu.make_async_copy(att, blocks.at[ring.own], local.at[0])
    for load in [*ups, *outs, own, lifted]:
        load.start()
    greet(ring.partners())
    ring.start(0, 1)
    for load in ups:
        load.wait()

    def merge(i):
        outs[i].wait()
        joint[pl.ds(i * 256, 256), :] = jnp.dot(wo_v[i], wu_v[...], preferred_element_type=F32).astype(BF16)

    def finish(r):
        ring.complete(r)
        cut = pl.ds(r * STEP, STEP)
        joined = jnp.concatenate([blocks[j, cut, :] for j in range(PARTS)], axis=1)
        raised = base_v[cut, :] + jnp.dot(joined, joint[...], preferred_element_type=F32)
        out[cut, :] = gelu(raised).astype(BF16)

    merge(0)
    merge(1)
    ring.start(1, 2)
    merge(2)
    merge(3)
    ring.forward(0)
    merge(4)
    ring.start(2, 3)
    merge(5)
    merge(6)
    ring.forward(1)
    ring.forward_far(0)
    merge(7)
    own.wait()
    lifted.wait()
    ring.forward(2)
    ring.forward_far(1)
    finish(0)
    ring.forward_far(2)
    finish(1)
    finish(2)
    ring.sent()


def expand(att, base, w_full, w_up):
    return pl.pallas_call(
        expand_kernel,
        out_shape=jax.ShapeDtypeStruct((TOK, KMER * HD), BF16),
        in_specs=[ANY] * 4,
        out_specs=VMEM,
        scratch_shapes=[
            pltpu.VMEM((PARTS, TOK, 256), BF16),
            pltpu.VMEM((PARTS, 256, D), BF16),
            pltpu.VMEM((D, KMER * HD), BF16),
            pltpu.VMEM((TOK, KMER * HD), F32),
            pltpu.VMEM((PARTS * 256, KMER * HD), BF16),
            pltpu.SemaphoreType.DMA((16,)),
            *gather_sems(CHUNKS),
        ],
        compiler_params=pltpu.CompilerParams(
            collective_id=2, has_side_effects=True, vmem_limit_bytes=56 << 20
        ),
    )(att, base, w_full, w_up)


def place_kernel(starts, lengths, expanded, w_class, own, lead, logits, lead_logits, wide, placed, classes):
    for j in range(KMER):
        wide[pl.ds(j, TOK, stride=8), :] = expanded[:, j * HD : (j + 1) * HD].astype(F32)
    placed[:LEAD, :] = jnp.zeros((LEAD, HD), F32)
    placed[NUC:, :] = jnp.zeros((LEAD + 16, HD), F32)
    classes[...] = jnp.zeros(classes.shape, F32)
    classes[:CLASSES, :] = w_class[...].astype(F32)
    shift = LEAD - lax.axis_index("seq") * NUC

    def one(t, carry):
        placed[pl.ds(starts[t] + shift, 8), :] = wide[pl.ds(pl.multiple_of(t * 8, 8), 8), :]
        return carry

    lax.fori_loop(0, TOK, one, 0, unroll=8)
    end = starts[TOK - 1] + lengths[TOK - 1] + shift
    placed[pl.ds(end, 8), :] = jnp.zeros((8, HD), F32)
    first = placed[:LEAD, :].astype(BF16)
    lead[...] = first
    rows = placed[LEAD : LEAD + NUC, :].astype(BF16)
    own[...] = rows
    spread = classes[...].astype(BF16)
    partial = lax.dot_general(spread, rows, NT, preferred_element_type=F32).astype(BF16)
    for j in range(PARTS - 1):
        logits[j] = partial[:, j * PIECE : (j + 1) * PIECE]
    rest = NUC - (PARTS - 1) * PIECE
    logits[PARTS - 1, :, :rest] = partial[:, (PARTS - 1) * PIECE :]
    logits[PARTS - 1, :, rest:] = jnp.zeros((16, PIECE - rest), BF16)
    lead_logits[...] = lax.dot_general(spread, first, NT, preferred_element_type=F32).astype(BF16)


def place(starts, lengths, expanded, w_class):
    return pl.pallas_call(
        place_kernel,
        out_shape=(
            jax.ShapeDtypeStruct((NUC, HD), BF16),
            jax.ShapeDtypeStruct((LEAD, HD), BF16),
            jax.ShapeDtypeStruct((PARTS, 16, PIECE), BF16),
            jax.ShapeDtypeStruct((16, LEAD), BF16),
        ),
        in_specs=[SMEM, SMEM, VMEM, VMEM],
        out_specs=(VMEM, VMEM, VMEM, VMEM),
        scratch_shapes=[
            pltpu.VMEM((TOK * 8, HD), F32),
            pltpu.VMEM((LEAD + NUC + 16, HD), F32),
            pltpu.VMEM((16, HD), F32),
        ],
        compiler_params=pltpu.CompilerParams(vmem_limit_bytes=48 << 20),
    )(starts, lengths, expanded, w_class)


def loss_kernel(
    lead, pieces, lead_logits, labels, arriving, loss,
    received, early, late, total, lab, mine, lead_ss, lead_rs, p_ss, p_rs, e_ss, e_rs, t_ss, t_rs, a_ss, a_rs, lab_sem,
):
    seq = lax.axis_index("seq")
    mp = lax.axis_index("mp")
    before, after = (seq + 15) % 16, (seq + 1) % 16
    others = [{"seq": seq, "mp": (mp + d) % PARTS} for d in range(1, PARTS)]
    head = NUC - (PARTS - 1) * PIECE
    split = (PARTS - 1) * PIECE - (NUC - LEAD)
    lab_head = pltpu.make_async_copy(
        labels.at[:, pl.ds(pl.multiple_of(mp * PIECE, PIECE), head)], lab.at[:, pl.ds(0, head)], lab_sem.at[0]
    )
    lab_tail = pltpu.make_async_copy(
        labels.at[:, pl.ds(pl.multiple_of(jnp.minimum(mp, PARTS - 2) * PIECE + head, HD), PIECE - head)],
        lab.at[:, pl.ds(head, PIECE - head)], lab_sem.at[1],
    )
    lab_head.start()
    lab_tail.start()

    barrier = pltpu.get_barrier_semaphore()
    for other in others + [{"seq": after, "mp": mp}]:
        pl.semaphore_signal(barrier, inc=1, device_id=other, device_id_type=MESH)

    @pl.when(mp >= PARTS - 2)
    def _():
        for j in range(PARTS):
            pl.semaphore_signal(barrier, inc=1, device_id={"seq": after, "mp": j}, device_id_type=MESH)

    pl.semaphore_wait(barrier, PARTS + 2)

    def piece(d):
        return remote(
            pieces.at[(mp + d) % PARTS], received.at[d - 1], p_ss.at[d - 1], p_rs.at[d - 1], others[d - 1]
        )

    def early_copy(slot):
        return remote(
            lead_logits.at[:, pl.ds(0, split)], early.at[slot], e_ss, e_rs.at[slot], {"seq": before, "mp": PARTS - 2}
        )

    def late_copy(slot):
        return remote(
            lead_logits.at[:, pl.ds(split, head)], late.at[slot], t_ss, t_rs.at[slot], {"seq": before, "mp": PARTS - 1}
        )

    early_copy(mp).start()
    late_copy(mp).start()
    for d in range(1, PARTS):
        piece(d).start()
    shift = remote(lead, arriving, lead_ss, lead_rs, {"seq": before, "mp": mp})
    shift.start()
    lab_head.wait()
    lab_tail.wait()
    for d in range(1, PARTS):
        piece(d).wait_recv()
    summed = pieces[mp].astype(F32)
    for d in range(1, PARTS):
        summed = summed + received[d - 1].astype(F32)
    total[...] = summed

    @pl.when(mp == PARTS - 2)
    def _():
        for j in range(PARTS):
            early_copy(j).wait_recv()
        for j in range(PARTS):
            total[:, PIECE - split :] = total[:, PIECE - split :] + early[j].astype(F32)

    @pl.when(mp == PARTS - 1)
    def _():
        for j in range(PARTS):
            late_copy(j).wait_recv()
        for j in range(PARTS):
            total[:, :head] = total[:, :head] + late[j].astype(F32)

    logit = total[:CLASSES, :]
    softplus = jnp.maximum(logit, 0.0) + jnp.log(1.0 + jnp.exp(-jnp.abs(logit)))
    terms = softplus - lab[...].astype(F32) * logit
    mine[...] = jnp.broadcast_to(jnp.sum(terms, axis=0, keepdims=True), (8, PIECE))

    def spread(d):
        return remote(mine, loss.at[mp], a_ss.at[d - 1], a_rs.at[d - 1], others[d - 1])

    for d in range(1, PARTS):
        spread(d).start()
    loss[mp] = mine[...]
    for d in range(1, PARTS):
        spread(d).wait_recv()
    shift.wait()
    early_copy(mp).wait_send()
    late_copy(mp).wait_send()
    for d in range(1, PARTS):
        piece(d).wait_send()
        spread(d).wait_send()


def losses(lead, pieces, lead_logits, labels):
    dma = pltpu.SemaphoreType.DMA
    head = NUC - (PARTS - 1) * PIECE
    return pl.pallas_call(
        loss_kernel,
        out_shape=(
            jax.ShapeDtypeStruct((LEAD, HD), BF16),
            jax.ShapeDtypeStruct((PARTS, 8, PIECE), F32),
        ),
        in_specs=[VMEM, VMEM, VMEM, ANY],
        out_specs=(VMEM, VMEM),
        scratch_shapes=[
            pltpu.VMEM((PARTS - 1, 16, PIECE), BF16),
            pltpu.VMEM((PARTS, 16, LEAD - head), BF16),
            pltpu.VMEM((PARTS, 16, head), BF16),
            pltpu.VMEM((16, PIECE), F32),
            pltpu.VMEM((CLASSES, PIECE), jnp.int32),
            pltpu.VMEM((8, PIECE), F32),
            dma, dma, dma((7,)), dma((7,)), dma, dma((PARTS,)), dma, dma((PARTS,)), dma((7,)), dma((7,)), dma((2,)),
        ],
        compiler_params=pltpu.CompilerParams(
            collective_id=3, has_side_effects=True, vmem_limit_bytes=32 << 20
        ),
    )(lead, pieces, lead_logits, labels)


def per_device(
    tokens, norm_gain, w_query, w_key, w_value, w_out, w_up, w_class, starts, lengths, labels
):
    att, w_full, base = attend(tokens.T, norm_gain.reshape(D // HD, HD), w_query, w_key, w_value, w_out, w_up)
    expanded = expand(att, base, w_full, w_up)
    own, lead, logits, lead_logits = place(starts, lengths, expanded, w_class.T)
    arriving, loss = losses(lead, logits, lead_logits, labels.T)
    features = own.at[NUC - LEAD :].add(arriving)
    return (features, loss[:, 0, :].reshape(-1)[:NUC])


def solution(mesh):
    return jax.shard_map(
        per_device,
        mesh=mesh,
        in_specs=(
            P("seq", "mp"),
            P(),
            P(None, "mp"),
            P(None, "mp"),
            P(None, "mp"),
            P("mp", None),
            P(None, None, "mp"),
            P("mp", None),
            P("seq"),
            P("seq"),
            P("seq", None),
        ),
        out_specs=(P("seq", "mp"), P("seq")),
        check_vma=False,
    )
```

```python
import functools
import math

import jax
import jax.numpy as jnp
from jax import lax
from jax.experimental import pallas as pl
from jax.experimental.pallas import tpu as pltpu
from jax.sharding import PartitionSpec as P

HD = 128
KMER = 6
TOK = 768
D = 2560
NUC = 3968
LEAD = 640
PIECE = 512
PARTS = 8
CLASSES = 14
MESH = pl.DeviceIdType.MESH
ANY = pl.BlockSpec(memory_space=pl.ANY)
VMEM = pl.BlockSpec(memory_space=pltpu.VMEM)
SMEM = pl.BlockSpec(memory_space=pltpu.SMEM)
BF16 = jnp.bfloat16
F32 = jnp.float32
NT = (((1,), (1,)), ((), ()))


def coords():
    seq = lax.axis_index("seq")
    mp = lax.axis_index("mp")
    return seq // 4, mp // 2, seq % 4, mp % 2


def device(x, y, z, core):
    return {"seq": x * 4 + z, "mp": y * 2 + core}


def greet(partners):
    barrier = pltpu.get_barrier_semaphore()
    for partner in partners:
        pl.semaphore_signal(barrier, inc=1, device_id=partner, device_id_type=MESH)
    pl.semaphore_wait(barrier, len(partners))


def remote(src, dst, send_sem, recv_sem, target):
    return pltpu.make_async_remote_copy(
        src_ref=src, dst_ref=dst, send_sem=send_sem, recv_sem=recv_sem, device_id=target, device_id_type=MESH
    )


class Gather:
    def __init__(self, src, buf, extent, chunks, y_send, y_recv, f_send, f_recv, c_send, c_recv, wide=0):
        self.src, self.buf, self.step, self.wide = src, buf, extent // chunks, wide
        self.chunks = chunks
        self.sems = (y_send, y_recv, f_send, f_recv, c_send, c_recv)
        x, y, z, core = coords()
        up, down, far = (y + 1) % 4, (y + 3) % 4, (y + 2) % 4
        self.up, self.down = device(x, up, z, core), device(x, down, z, core)
        self.sibling = device(x, y, z, 1 - core)
        self.own = y * 2 + core
        self.slots = [y * 2 + core, down * 2 + core, up * 2 + core, far * 2 + core]
        self.twins = [y * 2 + 1 - core, down * 2 + 1 - core, up * 2 + 1 - core, far * 2 + 1 - core]

    def partners(self):
        return [self.up, self.down, self.sibling]

    def cut(self, r, part):
        if part is None:
            return pl.ds(r * self.step, self.step)
        half = self.step // 2
        return pl.ds(r * self.step + part * half, half)

    def mine(self, r):
        cut = self.cut(r, None)
        return self.src.at[:, cut] if self.wide else self.src.at[cut]

    def at(self, slot, r, part=None):
        cut = self.cut(r, part)
        if self.wide:
            return self.buf.at[pl.ds(pl.multiple_of(slot * self.wide, 16), self.wide), cut]
        return self.buf.at[slot, cut]

    def toward(self, way):
        return self.up if way == 0 else self.down

    def around(self, way, r):
        y_send, y_recv = self.sems[:2]
        return remote(self.mine(r), self.at(self.own, r), y_send.at[way, r], y_recv.at[way, r], self.toward(way))

    def arrived(self, way, r):
        y_send, y_recv = self.sems[:2]
        slot = self.at(self.slots[1 + way], r)
        return remote(slot, slot, y_send.at[way, r], y_recv.at[way, r], self.toward(way))

    def onward(self, way, r):
        f_send, f_recv = self.sems[2:4]
        slot = self.at(self.slots[1 + way], r, way)
        return remote(slot, slot, f_send.at[way, r], f_recv.at[way, r], self.toward(way))

    def far_arrived(self, way, r):
        f_send, f_recv = self.sems[2:4]
        slot = self.at(self.slots[3], r, way)
        return remote(slot, slot, f_send.at[way, r], f_recv.at[way, r], self.toward(way))

    def across(self, which, r, arriving=False):
        c_send, c_recv = self.sems[4:]
        part = which - 3 if which >= 3 else None
        slots = self.twins if arriving else self.slots
        slot = self.at(slots[min(which, 3)], r, part)
        src = self.mine(r) if which == 0 and not arriving else slot
        return remote(src, slot, c_send.at[which, r], c_recv.at[which, r], self.sibling)

    def start(self, first=0, last=None):
        for r in range(first, self.chunks if last is None else last):
            self.around(0, r).start()
            self.around(1, r).start()
            self.across(0, r).start()

    def forward(self, r):
        for way in range(2):
            self.arrived(way, r).wait_recv()
            self.onward(way, r).start()
            self.across(1 + way, r).start()

    def forward_far(self, r):
        for way in range(2):
            self.far_arrived(way, r).wait_recv()
            self.across(3 + way, r).start()

    def complete(self, r):
        for which in range(5):
            self.across(which, r, arriving=True).wait_recv()

    def sent(self):
        for r in range(self.chunks):
            for way in range(2):
                self.around(way, r).wait_send()
                self.onward(way, r).wait_send()
            for which in range(5):
                self.across(which, r).wait_send()


def gather_sems(chunks):
    dma = pltpu.SemaphoreType.DMA
    return [dma((2, chunks)), dma((2, chunks)), dma((2, chunks)), dma((2, chunks)), dma((5, chunks)), dma((5, chunks))]


def pick(index, options):
    value = options[-1]
    for i in range(len(options) - 2, -1, -1):
        value = jnp.where(index == i, options[i], value)
    return value


CHUNKS = 3
STEP = TOK // CHUNKS
PARTS_W = 4
UNITS = [
    (0, 0), (1, 0), (2, 0), (1, 1), (2, 1), (1, 2), (2, 2), (0, 1),
    (3, 0), (3, 1), (3, 2), (3, 3), (1, 3), (2, 3), (0, 2), (0, 3),
]


def attend_kernel(
    tokens, gain, w_query, w_key, w_value, w_out, w_up, att, w_full, base,
    xb, weights, turned, up_in, up_turned, gains, qb, kb, vb, acc, top, o_send, l_send, o_recv, l_recv,
    local, q_ss, q_rs, k_ss, k_rs, v_ss, v_rs, far_ss, far_rs, o_ss, o_rs, l_ss, l_rs, *sems,
):
    x, y, z, core = coords()
    tok_ring = Gather(tokens, xb, TOK, CHUNKS, *sems[:6], wide=D // PARTS)
    ring = Gather(w_out, w_full, 256, PARTS_W, *sems[6:])

    def along(axis, by):
        if axis == 0:
            return device((x + by + 4) % 4, y, z, core)
        return device(x, y, (z + by + 4) % 4, core)

    offsets = {1: 1, 2: -1, 3: 2}

    def move(kind, h, slot, r):
        target = along(1 - h if kind == "q" else h, -offsets[slot])
        part = pl.ds(r * STEP, STEP)
        if kind == "q":
            src, dst, ss, rs = qb.at[h, 0, :, part], qb.at[h, slot, :, part], q_ss, q_rs
        elif kind == "k":
            src, dst, ss, rs = kb.at[h, 0, part], kb.at[h, slot, part], k_ss, k_rs
        else:
            src, dst, ss, rs = vb.at[h, 0, :, part], vb.at[h, slot, :, part], v_ss, v_rs
        return remote(src, dst, ss.at[h, slot, r], rs.at[h, slot, r], target)

    def send(r):
        for kind in "qkv":
            for slot in (1, 2):
                for h in range(2):
                    move(kind, h, slot, r).start()

    def relay(kind, h, slot):
        target = along(1 - h if kind == "q" else h, -offsets[slot])
        part = pl.ds((slot - 1) * (TOK // 2), TOK // 2)
        n = "qkv".index(kind)
        buf = (qb, kb, vb)[n]
        if kind == "k":
            src, dst = buf.at[h, slot, part], buf.at[h, 3, part]
        else:
            src, dst = buf.at[h, slot, :, part], buf.at[h, 3, :, part]
        return remote(src, dst, far_ss.at[n, h, slot - 1], far_rs.at[n, h, slot - 1], target)

    def lift(r):
        cut = pl.ds(r * STEP, STEP)
        base[cut, :] = jnp.dot(up_turned[...], xb[:, cut], preferred_element_type=F32).T

    own = pltpu.make_async_copy(
        tokens, xb.at[pl.ds(pl.multiple_of(tok_ring.own * (D // PARTS), 16), D // PARTS)], local.at[0]
    )
    own.start()
    loads = [pltpu.make_async_copy(w, weights.at[i], local.at[1 + i]) for i, w in enumerate((w_query, w_key, w_value))]
    for load in loads:
        load.start()
    own_w = pltpu.make_async_copy(w_out, w_full.at[ring.own], local.at[4])
    own_w.start()
    ups = [pltpu.make_async_copy(w_up.at[j], up_in.at[:, pl.ds(j * HD, HD)], local.at[5 + j]) for j in range(KMER)]
    for load in ups:
        load.start()
    greet([along(a, by) for a in range(2) for by in (1, -1, 2)] + ring.partners())
    tok_ring.start(0, 1)
    for i in range(D // HD):
        gains[pl.ds(i * HD, HD), :] = jnp.broadcast_to(gain[pl.ds(i, 1), :], (HD, HD)).T

    def turn(i):
        loads[i].wait()
        for j in range(D // 256):
            turned[pl.ds(i * 256, 256), pl.ds(j * 256, 256)] = weights[i, pl.ds(j * 256, 256), :].T

    def turn_up(i):
        for j in range(D // 256):
            up_turned[pl.ds(i * 256, 256), pl.ds(j * 256, 256)] = up_in[pl.ds(j * 256, 256), pl.ds(i * 256, 256)].T

    scale = math.log2(math.e) / math.sqrt(HD)

    def heads(r):
        tok_ring.complete(r)
        cut = pl.ds(r * STEP, STEP)
        wide = xb[:, cut].astype(F32)
        centred = wide - jnp.mean(wide, axis=0, keepdims=True)
        variance = jnp.mean(centred * centred, axis=0, keepdims=True)
        column = jnp.concatenate([gains[...]] * (STEP // HD), axis=1)
        normed = (centred * lax.rsqrt(variance + 1e-05) * column).astype(BF16)
        qkv = jnp.dot(turned[...], normed, preferred_element_type=F32)
        for h in range(2):
            at = h * HD
            qb[h, 0, :, cut] = (qkv[at : at + HD] * scale).astype(BF16)
            kb[h, 0, cut, :] = qkv[256 + at : 256 + at + HD].T.astype(BF16)
            vb[h, 0, :, cut] = qkv[512 + at : 512 + at + HD].astype(BF16)
        send(r)

    turn(0)
    tok_ring.start(1, 2)
    turn(1)
    turn(2)
    own.wait()
    tok_ring.forward(0)
    tok_ring.start(2, 3)
    for load in ups:
        load.wait()
    turn_up(0)
    top[...] = jnp.full(top.shape, -1e30, F32)
    acc[...] = jnp.zeros(acc.shape, F32)
    tok_ring.forward(1)
    tok_ring.forward_far(0)
    turn_up(1)
    heads(0)
    tok_ring.forward(2)
    tok_ring.forward_far(1)
    ring.start()
    heads(1)
    tok_ring.forward_far(2)
    turn_up(2)
    heads(2)

    ones = jnp.ones((16, TOK), BF16)

    def partial(h, a):
        total = acc[h, a, HD : HD + 8, :]
        return acc[h, a, :HD, :] / total[:1], top[h, a] + jnp.log2(total)

    def give(h, slot):
        by = pick(slot - 1, [1, -1, 2])
        target = along(1 - h, by)
        return [
            remote(o_send.at[h, slot - 1], o_recv.at[h, slot - 1], o_ss.at[h, slot - 1], o_rs.at[h, slot - 1], target),
            remote(l_send.at[h, slot - 1], l_recv.at[h, slot - 1], l_ss.at[h, slot - 1], l_rs.at[h, slot - 1], target),
        ]

    def unit(i, carry):
        def arrivals(kinds, slot):
            for kind in kinds:
                for h in range(2):
                    for r in range(CHUNKS):
                        move(kind, h, slot, r).wait_recv()

        def arrivals(kinds, slot):
            for kind in kinds:
                for h in range(2):
                    for r in range(CHUNKS):
                        move(kind, h, slot, r).wait_recv()
                    relay(kind, h, slot).start()

        def far_arrivals(kinds):
            for kind in kinds:
                for h in range(2):
                    for slot in (1, 2):
                        relay(kind, h, slot).wait_recv()

        for index, kinds, slot in ((1, "q", 1), (2, "q", 2), (3, "kv", 1), (4, "kv", 2)):
            pl.when(i == index)(functools.partial(arrivals, kinds, slot))
        for index, kinds in ((8, "q"), (11, "kv")):
            pl.when(i == index)(functools.partial(far_arrivals, kinds))

        @pl.when(i == 1)
        def _():
            lift(0)
            lift(1)

        for r, index in enumerate((2, 5, 9, 12)):
            pl.when(i == index)(functools.partial(ring.forward, r))
        a = pick(i, [u[0] for u in UNITS])
        b = pick(i, [u[1] for u in UNITS])
        scores = [
            jnp.dot(kb[h, b], qb[h, a], preferred_element_type=F32) for h in range(2)
        ]
        for h in range(2):
            s = scores[h]
            before = top[h, a]
            now = jnp.maximum(before, jnp.max(s, axis=0, keepdims=True))
            weights = jnp.exp2(s - now[:1]).astype(BF16)
            factor = jnp.exp2(before - now)
            lhs = jnp.concatenate([vb[h, b], ones], axis=0)
            added = jnp.dot(lhs, weights, preferred_element_type=F32)
            acc[h, a] = acc[h, a] * factor[:1] + added
            top[h, a] = now

        @pl.when(jnp.logical_and(i >= 11, i < 14))
        def _():
            for h in range(2):
                value, level = partial(h, a)
                o_send[h, a - 1] = value.astype(BF16)
                l_send[h, a - 1] = level
                for copy in give(h, a):
                    copy.start()

        return carry

    lax.fori_loop(0, len(UNITS), unit, 0)
    lift(CHUNKS - 1)
    for r in range(PARTS_W):
        ring.forward_far(r)
    for h in range(2):
        value, level = partial(h, 0)
        for slot in range(1, 4):
            for copy in give(h, slot):
                copy.wait_recv()
        levels = [level] + [l_recv[h, i] for i in range(3)]
        highest = functools.reduce(jnp.maximum, levels)
        shares = [jnp.exp2(one - highest) for one in levels]
        total = functools.reduce(jnp.add, shares)
        shares = [share / total for share in shares]
        value = value * shares[0][:1]
        for i in range(3):
            value = value + o_recv[h, i].astype(F32) * shares[1 + i][:1]
        att[:, pl.ds(h * HD, HD)] = value.T.astype(BF16)
    own_w.wait()
    for r in range(PARTS_W):
        ring.complete(r)
    tok_ring.sent()
    ring.sent()
    for h in range(2):
        for slot in (1, 2):
            for kind in "qkv":
                for r in range(CHUNKS):
                    move(kind, h, slot, r).wait_send()
                relay(kind, h, slot).wait_send()
        for slot in range(1, 4):
            for copy in give(h, slot):
                copy.wait_send()


def attend(tokens, gain, w_query, w_key, w_value, w_out, w_up):
    dma = pltpu.SemaphoreType.DMA
    return pl.pallas_call(
        attend_kernel,
        out_shape=(
            jax.ShapeDtypeStruct((TOK, 256), BF16),
            jax.ShapeDtypeStruct((PARTS, 256, D), BF16),
            jax.ShapeDtypeStruct((TOK, KMER * HD), F32),
        ),
        in_specs=[ANY, VMEM, ANY, ANY, ANY, ANY, ANY],
        out_specs=(VMEM, ANY, VMEM),
        scratch_shapes=[
            pltpu.VMEM((D, TOK), BF16),
            pltpu.VMEM((3, D, 256), BF16),
            pltpu.VMEM((768, D), BF16),
            pltpu.VMEM((D, KMER * HD), BF16),
            pltpu.VMEM((KMER * HD, D), BF16),
            pltpu.VMEM((D, HD), F32),
            pltpu.VMEM((2, 4, HD, TOK), BF16),
            pltpu.VMEM((2, 4, TOK, HD), BF16),
            pltpu.VMEM((2, 4, HD, TOK), BF16),
            pltpu.VMEM((2, 4, HD + 16, TOK), F32),
            pltpu.VMEM((2, 4, 8, TOK), F32),
            pltpu.VMEM((2, 3, HD, TOK), BF16),
            pltpu.VMEM((2, 3, 8, TOK), F32),
            pltpu.VMEM((2, 3, HD, TOK), BF16),
            pltpu.VMEM((2, 3, 8, TOK), F32),
            dma((5 + KMER,)),
            *[dma((2, 4, CHUNKS)) for _ in range(6)],
            dma((3, 2, 2)),
            dma((3, 2, 2)),
            *[dma((2, 3)) for _ in range(4)],
            *gather_sems(CHUNKS),
            *gather_sems(PARTS_W),
        ],
        compiler_params=pltpu.CompilerParams(
            collective_id=0, has_side_effects=True, vmem_limit_bytes=56 << 20
        ),
    )(tokens, gain, w_query, w_key, w_value, w_out, w_up)


def gelu(x):
    return 0.5 * x * (1.0 + jnp.tanh(math.sqrt(2.0 / math.pi) * (x + 0.044715 * x * x * x)))


def expand_kernel(att, base, w_full, w_up, out, blocks, wo_v, wu_v, base_v, joint, local, *sems):
    ring = Gather(att, blocks, TOK, CHUNKS, *sems)
    ups = [pltpu.make_async_copy(w_up.at[j], wu_v.at[:, pl.ds(j * HD, HD)], local.at[2 + j]) for j in range(KMER)]
    outs = [pltpu.make_async_copy(w_full.at[j], wo_v.at[j], local.at[8 + j]) for j in range(PARTS)]
    lifted = pltpu.make_async_copy(base, base_v, local.at[1])
    own = pltpu.make_async_copy(att, blocks.at[ring.own], local.at[0])
    for load in [*ups, *outs, own, lifted]:
        load.start()
    greet(ring.partners())
    ring.start(0, 1)
    for load in ups:
        load.wait()

    def merge(i):
        outs[i].wait()
        joint[pl.ds(i * 256, 256), :] = jnp.dot(wo_v[i], wu_v[...], preferred_element_type=F32).astype(BF16)

    def finish(r):
        ring.complete(r)
        cut = pl.ds(r * STEP, STEP)
        joined = jnp.concatenate([blocks[j, cut, :] for j in range(PARTS)], axis=1)
        raised = base_v[cut, :] + jnp.dot(joined, joint[...], preferred_element_type=F32)
        out[cut, :] = gelu(raised).astype(BF16)

    merge(0)
    merge(1)
    ring.start(1, 2)
    merge(2)
    merge(3)
    ring.forward(0)
    merge(4)
    ring.start(2, 3)
    merge(5)
    merge(6)
    ring.forward(1)
    ring.forward_far(0)
    merge(7)
    own.wait()
    lifted.wait()
    ring.forward(2)
    ring.forward_far(1)
    finish(0)
    ring.forward_far(2)
    finish(1)
    finish(2)
    ring.sent()


def expand(att, base, w_full, w_up):
    return pl.pallas_call(
        expand_kernel,
        out_shape=jax.ShapeDtypeStruct((TOK, KMER * HD), BF16),
        in_specs=[ANY] * 4,
        out_specs=VMEM,
        scratch_shapes=[
            pltpu.VMEM((PARTS, TOK, 256), BF16),
            pltpu.VMEM((PARTS, 256, D), BF16),
            pltpu.VMEM((D, KMER * HD), BF16),
            pltpu.VMEM((TOK, KMER * HD), F32),
            pltpu.VMEM((PARTS * 256, KMER * HD), BF16),
            pltpu.SemaphoreType.DMA((16,)),
            *gather_sems(CHUNKS),
        ],
        compiler_params=pltpu.CompilerParams(
            collective_id=2, has_side_effects=True, vmem_limit_bytes=56 << 20
        ),
    )(att, base, w_full, w_up)


def place_kernel(starts, lengths, expanded, w_class, own, lead, logits, lead_logits, wide, placed, classes):
    for j in range(KMER):
        wide[pl.ds(j, TOK, stride=8), :] = expanded[:, j * HD : (j + 1) * HD].astype(F32)
    placed[:LEAD, :] = jnp.zeros((LEAD, HD), F32)
    placed[NUC:, :] = jnp.zeros((LEAD + 16, HD), F32)
    classes[...] = jnp.zeros(classes.shape, F32)
    classes[:CLASSES, :] = w_class[...].astype(F32)
    shift = LEAD - lax.axis_index("seq") * NUC

    def one(t, carry):
        placed[pl.ds(starts[t] + shift, 8), :] = wide[pl.ds(pl.multiple_of(t * 8, 8), 8), :]
        return carry

    lax.fori_loop(0, TOK, one, 0, unroll=8)
    end = starts[TOK - 1] + lengths[TOK - 1] + shift
    placed[pl.ds(end, 8), :] = jnp.zeros((8, HD), F32)
    first = placed[:LEAD, :].astype(BF16)
    lead[...] = first
    rows = placed[LEAD : LEAD + NUC, :].astype(BF16)
    own[...] = rows
    spread = classes[...].astype(BF16)
    partial = lax.dot_general(spread, rows, NT, preferred_element_type=F32).astype(BF16)
    for j in range(PARTS - 1):
        logits[j] = partial[:, j * PIECE : (j + 1) * PIECE]
    rest = NUC - (PARTS - 1) * PIECE
    logits[PARTS - 1, :, :rest] = partial[:, (PARTS - 1) * PIECE :]
    logits[PARTS - 1, :, rest:] = jnp.zeros((16, PIECE - rest), BF16)
    lead_logits[...] = lax.dot_general(spread, first, NT, preferred_element_type=F32).astype(BF16)


def place(starts, lengths, expanded, w_class):
    return pl.pallas_call(
        place_kernel,
        out_shape=(
            jax.ShapeDtypeStruct((NUC, HD), BF16),
            jax.ShapeDtypeStruct((LEAD, HD), BF16),
            jax.ShapeDtypeStruct((PARTS, 16, PIECE), BF16),
            jax.ShapeDtypeStruct((16, LEAD), BF16),
        ),
        in_specs=[SMEM, SMEM, VMEM, VMEM],
        out_specs=(VMEM, VMEM, VMEM, VMEM),
        scratch_shapes=[
            pltpu.VMEM((TOK * 8, HD), F32),
            pltpu.VMEM((LEAD + NUC + 16, HD), F32),
            pltpu.VMEM((16, HD), F32),
        ],
        compiler_params=pltpu.CompilerParams(vmem_limit_bytes=48 << 20),
    )(starts, lengths, expanded, w_class)


def loss_kernel(
    lead, pieces, lead_logits, labels, arriving, loss,
    received, early, late, total, lab, mine, lead_ss, lead_rs, p_ss, p_rs, e_ss, e_rs, t_ss, t_rs, a_ss, a_rs, lab_sem,
):
    seq = lax.axis_index("seq")
    mp = lax.axis_index("mp")
    before, after = (seq + 15) % 16, (seq + 1) % 16
    others = [{"seq": seq, "mp": (mp + d) % PARTS} for d in range(1, PARTS)]
    head = NUC - (PARTS - 1) * PIECE
    split = (PARTS - 1) * PIECE - (NUC - LEAD)
    lab_head = pltpu.make_async_copy(
        labels.at[:, pl.ds(pl.multiple_of(mp * PIECE, PIECE), head)], lab.at[:, pl.ds(0, head)], lab_sem.at[0]
    )
    lab_tail = pltpu.make_async_copy(
        labels.at[:, pl.ds(pl.multiple_of(jnp.minimum(mp, PARTS - 2) * PIECE + head, HD), PIECE - head)],
        lab.at[:, pl.ds(head, PIECE - head)], lab_sem.at[1],
    )
    lab_head.start()
    lab_tail.start()

    barrier = pltpu.get_barrier_semaphore()
    for other in others + [{"seq": after, "mp": mp}]:
        pl.semaphore_signal(barrier, inc=1, device_id=other, device_id_type=MESH)

    @pl.when(mp >= PARTS - 2)
    def _():
        for j in range(PARTS):
            pl.semaphore_signal(barrier, inc=1, device_id={"seq": after, "mp": j}, device_id_type=MESH)

    pl.semaphore_wait(barrier, PARTS + 2)

    def piece(d):
        return remote(
            pieces.at[(mp + d) % PARTS], received.at[d - 1], p_ss.at[d - 1], p_rs.at[d - 1], others[d - 1]
        )

    def early_copy(slot):
        return remote(
            lead_logits.at[:, pl.ds(0, split)], early.at[slot], e_ss, e_rs.at[slot], {"seq": before, "mp": PARTS - 2}
        )

    def late_copy(slot):
        return remote(
            lead_logits.at[:, pl.ds(split, head)], late.at[slot], t_ss, t_rs.at[slot], {"seq": before, "mp": PARTS - 1}
        )

    early_copy(mp).start()
    late_copy(mp).start()
    for d in range(1, PARTS):
        piece(d).start()
    shift = remote(lead, arriving, lead_ss, lead_rs, {"seq": before, "mp": mp})
    shift.start()
    lab_head.wait()
    lab_tail.wait()
    for d in range(1, PARTS):
        piece(d).wait_recv()
    summed = pieces[mp].astype(F32)
    for d in range(1, PARTS):
        summed = summed + received[d - 1].astype(F32)
    total[...] = summed

    @pl.when(mp == PARTS - 2)
    def _():
        for j in range(PARTS):
            early_copy(j).wait_recv()
        for j in range(PARTS):
            total[:, PIECE - split :] = total[:, PIECE - split :] + early[j].astype(F32)

    @pl.when(mp == PARTS - 1)
    def _():
        for j in range(PARTS):
            late_copy(j).wait_recv()
        for j in range(PARTS):
            total[:, :head] = total[:, :head] + late[j].astype(F32)

    logit = total[:CLASSES, :]
    softplus = jnp.maximum(logit, 0.0) + jnp.log(1.0 + jnp.exp(-jnp.abs(logit)))
    terms = softplus - lab[...].astype(F32) * logit
    mine[...] = jnp.broadcast_to(jnp.sum(terms, axis=0, keepdims=True), (8, PIECE))

    def spread(d):
        return remote(mine, loss.at[mp], a_ss.at[d - 1], a_rs.at[d - 1], others[d - 1])

    for d in range(1, PARTS):
        spread(d).start()
    loss[mp] = mine[...]
    for d in range(1, PARTS):
        spread(d).wait_recv()
    shift.wait()
    early_copy(mp).wait_send()
    late_copy(mp).wait_send()
    for d in range(1, PARTS):
        piece(d).wait_send()
        spread(d).wait_send()


def losses(lead, pieces, lead_logits, labels):
    dma = pltpu.SemaphoreType.DMA
    head = NUC - (PARTS - 1) * PIECE
    return pl.pallas_call(
        loss_kernel,
        out_shape=(
            jax.ShapeDtypeStruct((LEAD, HD), BF16),
            jax.ShapeDtypeStruct((PARTS, 8, PIECE), F32),
        ),
        in_specs=[VMEM, VMEM, VMEM, ANY],
        out_specs=(VMEM, VMEM),
        scratch_shapes=[
            pltpu.VMEM((PARTS - 1, 16, PIECE), BF16),
            pltpu.VMEM((PARTS, 16, LEAD - head), BF16),
            pltpu.VMEM((PARTS, 16, head), BF16),
            pltpu.VMEM((16, PIECE), F32),
            pltpu.VMEM((CLASSES, PIECE), jnp.int32),
            pltpu.VMEM((8, PIECE), F32),
            dma, dma, dma((7,)), dma((7,)), dma, dma((PARTS,)), dma, dma((PARTS,)), dma((7,)), dma((7,)), dma((2,)),
        ],
        compiler_params=pltpu.CompilerParams(
            collective_id=3, has_side_effects=True, vmem_limit_bytes=32 << 20
        ),
    )(lead, pieces, lead_logits, labels)


def per_device(
    tokens, norm_gain, w_query, w_key, w_value, w_out, w_up, w_class, starts, lengths, labels
):
    att, w_full, base = attend(tokens.T, norm_gain.reshape(D // HD, HD), w_query, w_key, w_value, w_out, w_up)
    expanded = expand(att, base, w_full, w_up)
    own, lead, logits, lead_logits = place(starts, lengths, expanded, w_class.T)
    arriving, loss = losses(lead, logits, lead_logits, labels.T)
    features = own.at[NUC - LEAD :].add(arriving)
    return (features, loss[:, 0, :].reshape(-1)[:NUC])


def solution(mesh):
    return jax.shard_map(
        per_device,
        mesh=mesh,
        in_specs=(
            P("seq", "mp"),
            P(),
            P(None, "mp"),
            P(None, "mp"),
            P(None, "mp"),
            P("mp", None),
            P(None, None, "mp"),
            P("mp", None),
            P("seq"),
            P("seq"),
            P("seq", None),
        ),
        out_specs=(P("seq", "mp"), P("seq")),
        check_vma=False,
    )
```

```python
import functools
import math

import jax
import jax.numpy as jnp
from jax import lax
from jax.experimental import pallas as pl
from jax.experimental.pallas import tpu as pltpu
from jax.sharding import PartitionSpec as P

HD = 128
KMER = 6
TOK = 768
D = 2560
NUC = 3968
LEAD = 640
PIECE = 512
PARTS = 8
CLASSES = 14
MESH = pl.DeviceIdType.MESH
ANY = pl.BlockSpec(memory_space=pl.ANY)
VMEM = pl.BlockSpec(memory_space=pltpu.VMEM)
SMEM = pl.BlockSpec(memory_space=pltpu.SMEM)
BF16 = jnp.bfloat16
F32 = jnp.float32
NT = (((1,), (1,)), ((), ()))


def coords():
    seq = lax.axis_index("seq")
    mp = lax.axis_index("mp")
    return seq // 4, mp // 2, seq % 4, mp % 2


def device(x, y, z, core):
    return {"seq": x * 4 + z, "mp": y * 2 + core}


def greet(partners):
    barrier = pltpu.get_barrier_semaphore()
    for partner in partners:
        pl.semaphore_signal(barrier, inc=1, device_id=partner, device_id_type=MESH)
    pl.semaphore_wait(barrier, len(partners))


def remote(src, dst, send_sem, recv_sem, target):
    return pltpu.make_async_remote_copy(
        src_ref=src, dst_ref=dst, send_sem=send_sem, recv_sem=recv_sem, device_id=target, device_id_type=MESH
    )


class Gather:
    def __init__(self, src, buf, extent, chunks, y_send, y_recv, f_send, f_recv, c_send, c_recv, wide=0):
        self.src, self.buf, self.step, self.wide = src, buf, extent // chunks, wide
        self.chunks = chunks
        self.sems = (y_send, y_recv, f_send, f_recv, c_send, c_recv)
        x, y, z, core = coords()
        up, down, far = (y + 1) % 4, (y + 3) % 4, (y + 2) % 4
        self.up, self.down = device(x, up, z, core), device(x, down, z, core)
        self.sibling = device(x, y, z, 1 - core)
        self.own = y * 2 + core
        self.slots = [y * 2 + core, down * 2 + core, up * 2 + core, far * 2 + core]
        self.twins = [y * 2 + 1 - core, down * 2 + 1 - core, up * 2 + 1 - core, far * 2 + 1 - core]

    def partners(self):
        return [self.up, self.down, self.sibling]

    def cut(self, r):
        return pl.ds(r * self.step, self.step)

    def mine(self, r):
        cut = self.cut(r)
        return self.src.at[:, cut] if self.wide else self.src.at[cut]

    def at(self, slot, r):
        cut = self.cut(r)
        if self.wide:
            return self.buf.at[pl.ds(pl.multiple_of(slot * self.wide, 16), self.wide), cut]
        return self.buf.at[slot, cut]

    def toward(self, way):
        return self.up if way == 0 else self.down

    def around(self, way, r):
        y_send, y_recv = self.sems[:2]
        return remote(self.mine(r), self.at(self.own, r), y_send.at[way, r], y_recv.at[way, r], self.toward(way))

    def arrived(self, way, r):
        y_send, y_recv = self.sems[:2]
        slot = self.at(self.slots[1 + way], r)
        return remote(slot, slot, y_send.at[way, r], y_recv.at[way, r], self.toward(way))

    def onward(self, r):
        f_send, f_recv = self.sems[2:4]
        slot = self.at(self.slots[1 + r % 2], r)
        return remote(slot, slot, f_send.at[r], f_recv.at[r], self.toward(r % 2))

    def far_arrived(self, r):
        f_send, f_recv = self.sems[2:4]
        slot = self.at(self.slots[3], r)
        return remote(slot, slot, f_send.at[r], f_recv.at[r], self.toward(r % 2))

    def across(self, which, r, arriving=False):
        c_send, c_recv = self.sems[4:]
        slot = self.at((self.twins if arriving else self.slots)[which], r)
        src = self.mine(r) if which == 0 and not arriving else slot
        return remote(src, slot, c_send.at[which, r], c_recv.at[which, r], self.sibling)

    def start(self, first=0, last=None):
        for r in range(first, self.chunks if last is None else last):
            self.around(0, r).start()
            self.around(1, r).start()
            self.across(0, r).start()

    def forward(self, r):
        for way in (r % 2, 1 - r % 2):
            self.arrived(way, r).wait_recv()
            if way == r % 2:
                self.onward(r).start()
            self.across(1 + way, r).start()

    def forward_far(self, r):
        self.far_arrived(r).wait_recv()
        self.across(3, r).start()

    def complete(self, r):
        for which in range(4):
            self.across(which, r, arriving=True).wait_recv()

    def sent(self):
        for r in range(self.chunks):
            for way in range(2):
                self.around(way, r).wait_send()
            self.onward(r).wait_send()
            for which in range(4):
                self.across(which, r).wait_send()


def gather_sems(chunks):
    dma = pltpu.SemaphoreType.DMA
    return [dma((2, chunks)), dma((2, chunks)), dma((chunks,)), dma((chunks,)), dma((4, chunks)), dma((4, chunks))]


def pick(index, options):
    value = options[-1]
    for i in range(len(options) - 2, -1, -1):
        value = jnp.where(index == i, options[i], value)
    return value


CHUNKS = 3
RING = 2 * CHUNKS
STEP = TOK // CHUNKS
PARTS_W = 4
UNITS = [
    (0, 0), (1, 0), (2, 0), (1, 1), (2, 1), (1, 2), (2, 2), (3, 0),
    (3, 1), (3, 2), (3, 3), (1, 3), (2, 3), (0, 1), (0, 2), (0, 3),
]


def attend_kernel(
    tokens, gain, w_query, w_key, w_value, w_out, w_up, att, w_full, base,
    xb, weights, turned, up_in, gains, qb, kb, vb, acc, top, o_send, l_send, o_recv, l_recv,
    local, q_ss, q_rs, k_ss, k_rs, v_ss, v_rs, far_ss, far_rs, o_ss, o_rs, l_ss, l_rs, *sems,
):
    x, y, z, core = coords()
    tok_ring = Gather(tokens, xb, TOK, RING, *sems[:6], wide=D // PARTS)
    ring = Gather(w_out, w_full, 256, PARTS_W, *sems[6:])

    def along(axis, by):
        if axis == 0:
            return device((x + by + 4) % 4, y, z, core)
        return device(x, y, (z + by + 4) % 4, core)

    offsets = {1: 1, 2: -1, 3: 2}

    def move(kind, h, slot, r):
        target = along(1 - h if kind == "q" else h, -offsets[slot])
        part = pl.ds(r * STEP, STEP)
        if kind == "q":
            src, dst, ss, rs = qb.at[h, 0, :, part], qb.at[h, slot, :, part], q_ss, q_rs
        elif kind == "k":
            src, dst, ss, rs = kb.at[h, 0, part], kb.at[h, slot, part], k_ss, k_rs
        else:
            src, dst, ss, rs = vb.at[h, 0, :, part], vb.at[h, slot, :, part], v_ss, v_rs
        return remote(src, dst, ss.at[h, slot, r], rs.at[h, slot, r], target)

    def send(r):
        for kind in "qkv":
            for slot in (1, 2):
                for h in range(2):
                    move(kind, h, slot, r).start()

    def relay(kind, h, slot):
        target = along(1 - h if kind == "q" else h, -offsets[slot])
        part = pl.ds((slot - 1) * (TOK // 2), TOK // 2)
        n = "qkv".index(kind)
        buf = (qb, kb, vb)[n]
        if kind == "k":
            src, dst = buf.at[h, slot, part], buf.at[h, 3, part]
        else:
            src, dst = buf.at[h, slot, :, part], buf.at[h, 3, :, part]
        return remote(src, dst, far_ss.at[n, h, slot - 1], far_rs.at[n, h, slot - 1], target)

    def lift(r):
        cut = pl.ds(r * STEP, STEP)
        base[cut, :] = jnp.dot(xb[:, cut].T, up_in[...], preferred_element_type=F32)

    own = pltpu.make_async_copy(
        tokens, xb.at[pl.ds(pl.multiple_of(tok_ring.own * (D // PARTS), 16), D // PARTS)], local.at[0]
    )
    own.start()
    loads = [pltpu.make_async_copy(w, weights.at[i], local.at[1 + i]) for i, w in enumerate((w_query, w_key, w_value))]
    for load in loads:
        load.start()
    own_w = pltpu.make_async_copy(w_out, w_full.at[ring.own], local.at[4])
    own_w.start()
    ups = [pltpu.make_async_copy(w_up.at[j], up_in.at[:, pl.ds(j * HD, HD)], local.at[5 + j]) for j in range(KMER)]
    for load in ups:
        load.start()
    greet([along(a, by) for a in range(2) for by in (1, -1, 2)] + ring.partners())
    tok_ring.start(0, 3)
    for i in range(D // HD):
        gains[pl.ds(i * HD, HD), :] = jnp.broadcast_to(gain[pl.ds(i, 1), :], (HD, HD)).T

    def turn(i):
        loads[i].wait()
        for j in range(D // 256):
            turned[pl.ds(i * 256, 256), pl.ds(j * 256, 256)] = weights[i, pl.ds(j * 256, 256), :].T

    scale = math.log2(math.e) / math.sqrt(HD)

    def heads(r):
        tok_ring.complete(2 * r)
        tok_ring.complete(2 * r + 1)
        cut = pl.ds(r * STEP, STEP)
        wide = xb[:, cut].astype(F32)
        centred = wide - jnp.mean(wide, axis=0, keepdims=True)
        variance = jnp.mean(centred * centred, axis=0, keepdims=True)
        column = jnp.concatenate([gains[...]] * (STEP // HD), axis=1)
        normed = (centred * lax.rsqrt(variance + 1e-05) * column).astype(BF16)
        qkv = jnp.dot(turned[...], normed, preferred_element_type=F32)
        for h in range(2):
            at = h * HD
            qb[h, 0, :, cut] = (qkv[at : at + HD] * scale).astype(BF16)
            kb[h, 0, cut, :] = qkv[256 + at : 256 + at + HD].T.astype(BF16)
            vb[h, 0, :, cut] = qkv[512 + at : 512 + at + HD].astype(BF16)
        send(r)

    for i in range(3):
        turn(i)
    top[...] = jnp.full(top.shape, -1e30, F32)
    acc[...] = jnp.zeros(acc.shape, F32)
    own.wait()
    for r in range(3):
        tok_ring.forward(r)
        tok_ring.start(r + 3, r + 4)
    tok_ring.forward_far(0)
    tok_ring.forward(3)
    tok_ring.forward_far(1)
    heads(0)
    tok_ring.forward(4)
    tok_ring.forward_far(2)
    tok_ring.forward(5)
    tok_ring.forward_far(3)
    ring.start()
    heads(1)
    for load in ups:
        load.wait()
    lift(0)
    tok_ring.forward_far(4)
    tok_ring.forward_far(5)
    heads(2)

    ones = jnp.ones((16, TOK), BF16)

    def partial(h, a):
        total = acc[h, a, HD : HD + 8, :]
        return acc[h, a, :HD, :] / total[:1], top[h, a] + jnp.log2(total)

    def give(h, slot):
        by = pick(slot - 1, [1, -1, 2])
        target = along(1 - h, by)
        return [
            remote(o_send.at[h, slot - 1], o_recv.at[h, slot - 1], o_ss.at[h, slot - 1], o_rs.at[h, slot - 1], target),
            remote(l_send.at[h, slot - 1], l_recv.at[h, slot - 1], l_ss.at[h, slot - 1], l_rs.at[h, slot - 1], target),
        ]

    def unit(i, carry):
        def arrivals(kinds, slot):
            for kind in kinds:
                for h in range(2):
                    for r in range(CHUNKS):
                        move(kind, h, slot, r).wait_recv()

        def arrivals(kinds, slot):
            for kind in kinds:
                for h in range(2):
                    for r in range(CHUNKS):
                        move(kind, h, slot, r).wait_recv()
                    relay(kind, h, slot).start()

        def far_arrivals(kinds):
            for kind in kinds:
                for h in range(2):
                    for slot in (1, 2):
                        relay(kind, h, slot).wait_recv()

        for index, kinds, slot in ((1, "q", 1), (2, "q", 2), (3, "kv", 1), (4, "kv", 2)):
            pl.when(i == index)(functools.partial(arrivals, kinds, slot))
        for index, kinds in ((7, "q"), (10, "kv")):
            pl.when(i == index)(functools.partial(far_arrivals, kinds))

        @pl.when(i == 1)
        def _():
            lift(1)

        for step, index, pair in (
            (ring.forward, 9, 0), (ring.forward, 10, 1), (ring.forward_far, 14, 0),
        ):
            @pl.when(i == index)
            def _(step=step, pair=pair):
                step(2 * pair)
                step(2 * pair + 1)

        a = pick(i, [u[0] for u in UNITS])
        b = pick(i, [u[1] for u in UNITS])
        scores = [
            jnp.dot(kb[h, b], qb[h, a], preferred_element_type=F32) for h in range(2)
        ]
        for h in range(2):
            s = scores[h]
            before = top[h, a]
            now = jnp.maximum(before, jnp.max(s, axis=0, keepdims=True))
            weights = jnp.exp2(s - now[:1]).astype(BF16)
            factor = jnp.exp2(before - now)
            lhs = jnp.concatenate([vb[h, b], ones], axis=0)
            added = jnp.dot(lhs, weights, preferred_element_type=F32)
            acc[h, a] = acc[h, a] * factor[:1] + added
            top[h, a] = now

        @pl.when(jnp.logical_and(i >= 10, i < 13))
        def _():
            for h in range(2):
                value, level = partial(h, a)
                o_send[h, a - 1] = value.astype(BF16)
                l_send[h, a - 1] = level
                for copy in give(h, a):
                    copy.start()

        return carry

    lax.fori_loop(0, len(UNITS), unit, 0)
    lift(CHUNKS - 1)
    for r in range(PARTS_W - 2, PARTS_W):
        ring.forward_far(r)
    for h in range(2):
        value, level = partial(h, 0)
        for slot in range(1, 4):
            for copy in give(h, slot):
                copy.wait_recv()
        levels = [level] + [l_recv[h, i] for i in range(3)]
        highest = functools.reduce(jnp.maximum, levels)
        shares = [jnp.exp2(one - highest) for one in levels]
        total = functools.reduce(jnp.add, shares)
        shares = [share / total for share in shares]
        value = value * shares[0][:1]
        for i in range(3):
            value = value + o_recv[h, i].astype(F32) * shares[1 + i][:1]
        att[:, pl.ds(h * HD, HD)] = value.T.astype(BF16)
    own_w.wait()
    for r in range(PARTS_W):
        ring.complete(r)
    tok_ring.sent()
    ring.sent()
    for h in range(2):
        for slot in (1, 2):
            for kind in "qkv":
                for r in range(CHUNKS):
                    move(kind, h, slot, r).wait_send()
                relay(kind, h, slot).wait_send()
        for slot in range(1, 4):
            for copy in give(h, slot):
                copy.wait_send()


def attend(tokens, gain, w_query, w_key, w_value, w_out, w_up):
    dma = pltpu.SemaphoreType.DMA
    return pl.pallas_call(
        attend_kernel,
        out_shape=(
            jax.ShapeDtypeStruct((TOK, 256), BF16),
            jax.ShapeDtypeStruct((PARTS, 256, D), BF16),
            jax.ShapeDtypeStruct((TOK, KMER * HD), F32),
        ),
        in_specs=[ANY, VMEM, ANY, ANY, ANY, ANY, ANY],
        out_specs=(VMEM, ANY, VMEM),
        scratch_shapes=[
            pltpu.VMEM((D, TOK), BF16),
            pltpu.VMEM((3, D, 256), BF16),
            pltpu.VMEM((768, D), BF16),
            pltpu.VMEM((D, KMER * HD), BF16),
            pltpu.VMEM((D, HD), F32),
            pltpu.VMEM((2, 4, HD, TOK), BF16),
            pltpu.VMEM((2, 4, TOK, HD), BF16),
            pltpu.VMEM((2, 4, HD, TOK), BF16),
            pltpu.VMEM((2, 4, HD + 16, TOK), F32),
            pltpu.VMEM((2, 4, 8, TOK), F32),
            pltpu.VMEM((2, 3, HD, TOK), BF16),
            pltpu.VMEM((2, 3, 8, TOK), F32),
            pltpu.VMEM((2, 3, HD, TOK), BF16),
            pltpu.VMEM((2, 3, 8, TOK), F32),
            dma((5 + KMER,)),
            *[dma((2, 4, CHUNKS)) for _ in range(6)],
            dma((3, 2, 2)),
            dma((3, 2, 2)),
            *[dma((2, 3)) for _ in range(4)],
            *gather_sems(RING),
            *gather_sems(PARTS_W),
        ],
        compiler_params=pltpu.CompilerParams(
            collective_id=0, has_side_effects=True, vmem_limit_bytes=56 << 20
        ),
    )(tokens, gain, w_query, w_key, w_value, w_out, w_up)


def gelu(x):
    return 0.5 * x * (1.0 + jnp.tanh(math.sqrt(2.0 / math.pi) * (x + 0.044715 * x * x * x)))


def expand_kernel(att, base, w_full, w_up, out, blocks, wo_v, wu_v, base_v, joint, local, *sems):
    ring = Gather(att, blocks, TOK, RING, *sems)
    ups = [pltpu.make_async_copy(w_up.at[j], wu_v.at[:, pl.ds(j * HD, HD)], local.at[2 + j]) for j in range(KMER)]
    outs = [pltpu.make_async_copy(w_full.at[j], wo_v.at[j], local.at[8 + j]) for j in range(PARTS)]
    lifted = pltpu.make_async_copy(base, base_v, local.at[1])
    own = pltpu.make_async_copy(att, blocks.at[ring.own], local.at[0])
    for load in [*ups, *outs, own, lifted]:
        load.start()
    greet(ring.partners())
    ring.start(0, 3)
    for load in ups:
        load.wait()

    def merge(i):
        outs[i].wait()
        joint[pl.ds(i * 256, 256), :] = jnp.dot(wo_v[i], wu_v[...], preferred_element_type=F32).astype(BF16)

    def finish(r):
        ring.complete(2 * r)
        ring.complete(2 * r + 1)
        cut = pl.ds(r * STEP, STEP)
        joined = jnp.concatenate([blocks[j, cut, :] for j in range(PARTS)], axis=1)
        raised = base_v[cut, :] + jnp.dot(joined, joint[...], preferred_element_type=F32)
        out[cut, :] = gelu(raised).astype(BF16)

    for i in range(4):
        merge(i)
    for r in range(3):
        ring.forward(r)
        ring.start(r + 3, r + 4)
    merge(4)
    merge(5)
    ring.forward_far(0)
    ring.forward(3)
    ring.forward_far(1)
    merge(6)
    ring.forward(4)
    ring.forward_far(2)
    merge(7)
    own.wait()
    lifted.wait()
    ring.forward(5)
    ring.forward_far(3)
    finish(0)
    ring.forward_far(4)
    ring.forward_far(5)
    finish(1)
    finish(2)
    ring.sent()


def expand(att, base, w_full, w_up):
    return pl.pallas_call(
        expand_kernel,
        out_shape=jax.ShapeDtypeStruct((TOK, KMER * HD), BF16),
        in_specs=[ANY] * 4,
        out_specs=VMEM,
        scratch_shapes=[
            pltpu.VMEM((PARTS, TOK, 256), BF16),
            pltpu.VMEM((PARTS, 256, D), BF16),
            pltpu.VMEM((D, KMER * HD), BF16),
            pltpu.VMEM((TOK, KMER * HD), F32),
            pltpu.VMEM((PARTS * 256, KMER * HD), BF16),
            pltpu.SemaphoreType.DMA((16,)),
            *gather_sems(RING),
        ],
        compiler_params=pltpu.CompilerParams(
            collective_id=2, has_side_effects=True, vmem_limit_bytes=56 << 20
        ),
    )(att, base, w_full, w_up)


def place_kernel(starts, lengths, expanded, w_class, own, lead, logits, lead_logits, wide, placed, classes):
    for j in range(KMER):
        wide[pl.ds(j, TOK, stride=8), :] = expanded[:, j * HD : (j + 1) * HD].astype(F32)
    placed[:LEAD, :] = jnp.zeros((LEAD, HD), F32)
    placed[NUC:, :] = jnp.zeros((LEAD + 16, HD), F32)
    classes[...] = jnp.zeros(classes.shape, F32)
    classes[:CLASSES, :] = w_class[...].astype(F32)
    shift = LEAD - lax.axis_index("seq") * NUC

    def one(t, carry):
        placed[pl.ds(starts[t] + shift, 8), :] = wide[pl.ds(pl.multiple_of(t * 8, 8), 8), :]
        return carry

    lax.fori_loop(0, TOK, one, 0, unroll=8)
    end = starts[TOK - 1] + lengths[TOK - 1] + shift
    placed[pl.ds(end, 8), :] = jnp.zeros((8, HD), F32)
    first = placed[:LEAD, :].astype(BF16)
    lead[...] = first
    rows = placed[LEAD : LEAD + NUC, :].astype(BF16)
    own[...] = rows
    spread = classes[...].astype(BF16)
    partial = lax.dot_general(spread, rows, NT, preferred_element_type=F32).astype(BF16)
    for j in range(PARTS - 1):
        logits[j] = partial[:, j * PIECE : (j + 1) * PIECE]
    rest = NUC - (PARTS - 1) * PIECE
    logits[PARTS - 1, :, :rest] = partial[:, (PARTS - 1) * PIECE :]
    logits[PARTS - 1, :, rest:] = jnp.zeros((16, PIECE - rest), BF16)
    lead_logits[...] = lax.dot_general(spread, first, NT, preferred_element_type=F32).astype(BF16)


def place(starts, lengths, expanded, w_class):
    return pl.pallas_call(
        place_kernel,
        out_shape=(
            jax.ShapeDtypeStruct((NUC, HD), BF16),
            jax.ShapeDtypeStruct((LEAD, HD), BF16),
            jax.ShapeDtypeStruct((PARTS, 16, PIECE), BF16),
            jax.ShapeDtypeStruct((16, LEAD), BF16),
        ),
        in_specs=[SMEM, SMEM, VMEM, VMEM],
        out_specs=(VMEM, VMEM, VMEM, VMEM),
        scratch_shapes=[
            pltpu.VMEM((TOK * 8, HD), F32),
            pltpu.VMEM((LEAD + NUC + 16, HD), F32),
            pltpu.VMEM((16, HD), F32),
        ],
        compiler_params=pltpu.CompilerParams(vmem_limit_bytes=48 << 20),
    )(starts, lengths, expanded, w_class)


def loss_kernel(
    lead, pieces, lead_logits, labels, arriving, loss,
    received, early, late, total, lab, mine, lead_ss, lead_rs, p_ss, p_rs, e_ss, e_rs, t_ss, t_rs, a_ss, a_rs, lab_sem,
):
    seq = lax.axis_index("seq")
    mp = lax.axis_index("mp")
    before, after = (seq + 15) % 16, (seq + 1) % 16
    others = [{"seq": seq, "mp": (mp + d) % PARTS} for d in range(1, PARTS)]
    head = NUC - (PARTS - 1) * PIECE
    split = (PARTS - 1) * PIECE - (NUC - LEAD)
    lab_head = pltpu.make_async_copy(
        labels.at[:, pl.ds(pl.multiple_of(mp * PIECE, PIECE), head)], lab.at[:, pl.ds(0, head)], lab_sem.at[0]
    )
    lab_tail = pltpu.make_async_copy(
        labels.at[:, pl.ds(pl.multiple_of(jnp.minimum(mp, PARTS - 2) * PIECE + head, HD), PIECE - head)],
        lab.at[:, pl.ds(head, PIECE - head)], lab_sem.at[1],
    )
    lab_head.start()
    lab_tail.start()

    barrier = pltpu.get_barrier_semaphore()
    for other in others + [{"seq": after, "mp": mp}]:
        pl.semaphore_signal(barrier, inc=1, device_id=other, device_id_type=MESH)

    @pl.when(mp >= PARTS - 2)
    def _():
        for j in range(PARTS):
            pl.semaphore_signal(barrier, inc=1, device_id={"seq": after, "mp": j}, device_id_type=MESH)

    pl.semaphore_wait(barrier, PARTS + 2)

    def piece(d):
        return remote(
            pieces.at[(mp + d) % PARTS], received.at[d - 1], p_ss.at[d - 1], p_rs.at[d - 1], others[d - 1]
        )

    def early_copy(slot):
        return remote(
            lead_logits.at[:, pl.ds(0, split)], early.at[slot], e_ss, e_rs.at[slot], {"seq": before, "mp": PARTS - 2}
        )

    def late_copy(slot):
        return remote(
            lead_logits.at[:, pl.ds(split, head)], late.at[slot], t_ss, t_rs.at[slot], {"seq": before, "mp": PARTS - 1}
        )

    early_copy(mp).start()
    late_copy(mp).start()
    shift = remote(lead, arriving, lead_ss, lead_rs, {"seq": before, "mp": mp})
    shift.start()
    for d in range(1, PARTS):
        piece(d).start()
    lab_head.wait()
    lab_tail.wait()
    for d in range(1, PARTS):
        piece(d).wait_recv()
    summed = pieces[mp].astype(F32)
    for d in range(1, PARTS):
        summed = summed + received[d - 1].astype(F32)
    total[...] = summed

    @pl.when(mp == PARTS - 2)
    def _():
        for j in range(PARTS):
            early_copy(j).wait_recv()
        for j in range(PARTS):
            total[:, PIECE - split :] = total[:, PIECE - split :] + early[j].astype(F32)

    @pl.when(mp == PARTS - 1)
    def _():
        for j in range(PARTS):
            late_copy(j).wait_recv()
        for j in range(PARTS):
            total[:, :head] = total[:, :head] + late[j].astype(F32)

    logit = total[:CLASSES, :]
    softplus = jnp.maximum(logit, 0.0) + jnp.log(1.0 + jnp.exp(-jnp.abs(logit)))
    terms = softplus - lab[...].astype(F32) * logit
    mine[...] = jnp.broadcast_to(jnp.sum(terms, axis=0, keepdims=True), (8, PIECE))

    def spread(d):
        return remote(mine, loss.at[mp], a_ss.at[d - 1], a_rs.at[d - 1], others[d - 1])

    for d in range(1, PARTS):
        spread(d).start()
    loss[mp] = mine[...]
    for d in range(1, PARTS):
        spread(d).wait_recv()
    shift.wait()
    early_copy(mp).wait_send()
    late_copy(mp).wait_send()
    for d in range(1, PARTS):
        piece(d).wait_send()
        spread(d).wait_send()


def losses(lead, pieces, lead_logits, labels):
    dma = pltpu.SemaphoreType.DMA
    head = NUC - (PARTS - 1) * PIECE
    return pl.pallas_call(
        loss_kernel,
        out_shape=(
            jax.ShapeDtypeStruct((LEAD, HD), BF16),
            jax.ShapeDtypeStruct((PARTS, 8, PIECE), F32),
        ),
        in_specs=[VMEM, VMEM, VMEM, ANY],
        out_specs=(VMEM, VMEM),
        scratch_shapes=[
            pltpu.VMEM((PARTS - 1, 16, PIECE), BF16),
            pltpu.VMEM((PARTS, 16, LEAD - head), BF16),
            pltpu.VMEM((PARTS, 16, head), BF16),
            pltpu.VMEM((16, PIECE), F32),
            pltpu.VMEM((CLASSES, PIECE), jnp.int32),
            pltpu.VMEM((8, PIECE), F32),
            dma, dma, dma((7,)), dma((7,)), dma, dma((PARTS,)), dma, dma((PARTS,)), dma((7,)), dma((7,)), dma((2,)),
        ],
        compiler_params=pltpu.CompilerParams(
            collective_id=3, has_side_effects=True, vmem_limit_bytes=32 << 20
        ),
    )(lead, pieces, lead_logits, labels)


def per_device(
    tokens, norm_gain, w_query, w_key, w_value, w_out, w_up, w_class, starts, lengths, labels
):
    att, w_full, base = attend(tokens.T, norm_gain.reshape(D // HD, HD), w_query, w_key, w_value, w_out, w_up)
    expanded = expand(att, base, w_full, w_up)
    own, lead, logits, lead_logits = place(starts, lengths, expanded, w_class.T)
    arriving, loss = losses(lead, logits, lead_logits, labels.T)
    features = own.at[NUC - LEAD :].add(arriving)
    return (features, loss[:, 0, :].reshape(-1)[:NUC])


def solution(mesh):
    return jax.shard_map(
        per_device,
        mesh=mesh,
        in_specs=(
            P("seq", "mp"),
            P(),
            P(None, "mp"),
            P(None, "mp"),
            P(None, "mp"),
            P("mp", None),
            P(None, None, "mp"),
            P("mp", None),
            P("seq"),
            P("seq"),
            P("seq", None),
        ),
        out_specs=(P("seq", "mp"), P("seq")),
        check_vma=False,
    )
```

```python
import functools
import math

import jax
import jax.numpy as jnp
from jax import lax
from jax.experimental import pallas as pl
from jax.experimental.pallas import tpu as pltpu
from jax.sharding import PartitionSpec as P

HD = 128
KMER = 6
TOK = 768
D = 2560
NUC = 3968
LEAD = 640
PIECE = 512
PARTS = 8
CLASSES = 14
MESH = pl.DeviceIdType.MESH
ANY = pl.BlockSpec(memory_space=pl.ANY)
VMEM = pl.BlockSpec(memory_space=pltpu.VMEM)
SMEM = pl.BlockSpec(memory_space=pltpu.SMEM)
BF16 = jnp.bfloat16
F32 = jnp.float32
NT = (((1,), (1,)), ((), ()))


def coords():
    seq = lax.axis_index("seq")
    mp = lax.axis_index("mp")
    return seq // 4, mp // 2, seq % 4, mp % 2


def device(x, y, z, core):
    return {"seq": x * 4 + z, "mp": y * 2 + core}


def greet(partners):
    barrier = pltpu.get_barrier_semaphore()
    for partner in partners:
        pl.semaphore_signal(barrier, inc=1, device_id=partner, device_id_type=MESH)
    pl.semaphore_wait(barrier, len(partners))


def remote(src, dst, send_sem, recv_sem, target):
    return pltpu.make_async_remote_copy(
        src_ref=src, dst_ref=dst, send_sem=send_sem, recv_sem=recv_sem, device_id=target, device_id_type=MESH
    )


class Gather:
    def __init__(self, src, buf, extent, chunks, y_send, y_recv, f_send, f_recv, c_send, c_recv, wide=0):
        self.src, self.buf, self.step, self.wide = src, buf, extent // chunks, wide
        self.chunks = chunks
        self.sems = (y_send, y_recv, f_send, f_recv, c_send, c_recv)
        x, y, z, core = coords()
        up, down, far = (y + 1) % 4, (y + 3) % 4, (y + 2) % 4
        self.up, self.down = device(x, up, z, core), device(x, down, z, core)
        self.sibling = device(x, y, z, 1 - core)
        self.own = y * 2 + core
        self.slots = [y * 2 + core, down * 2 + core, up * 2 + core, far * 2 + core]
        self.twins = [y * 2 + 1 - core, down * 2 + 1 - core, up * 2 + 1 - core, far * 2 + 1 - core]

    def partners(self):
        return [self.up, self.down, self.sibling]

    def cut(self, r, part):
        if part is None:
            return pl.ds(r * self.step, self.step)
        half = self.step // 2
        return pl.ds(r * self.step + part * half, half)

    def mine(self, r):
        cut = self.cut(r, None)
        return self.src.at[:, cut] if self.wide else self.src.at[cut]

    def at(self, slot, r, part=None):
        cut = self.cut(r, part)
        if self.wide:
            return self.buf.at[pl.ds(pl.multiple_of(slot * self.wide, 16), self.wide), cut]
        return self.buf.at[slot, cut]

    def toward(self, way):
        return self.up if way == 0 else self.down

    def around(self, way, r):
        y_send, y_recv = self.sems[:2]
        return remote(self.mine(r), self.at(self.own, r), y_send.at[way, r], y_recv.at[way, r], self.toward(way))

    def arrived(self, way, r):
        y_send, y_recv = self.sems[:2]
        slot = self.at(self.slots[1 + way], r)
        return remote(slot, slot, y_send.at[way, r], y_recv.at[way, r], self.toward(way))

    def onward(self, way, r):
        f_send, f_recv = self.sems[2:4]
        slot = self.at(self.slots[1 + way], r, way)
        return remote(slot, slot, f_send.at[way, r], f_recv.at[way, r], self.toward(way))

    def far_arrived(self, way, r):
        f_send, f_recv = self.sems[2:4]
        slot = self.at(self.slots[3], r, way)
        return remote(slot, slot, f_send.at[way, r], f_recv.at[way, r], self.toward(way))

    def across(self, which, r, arriving=False):
        c_send, c_recv = self.sems[4:]
        part = which - 3 if which >= 3 else None
        slots = self.twins if arriving else self.slots
        slot = self.at(slots[min(which, 3)], r, part)
        src = self.mine(r) if which == 0 and not arriving else slot
        return remote(src, slot, c_send.at[which, r], c_recv.at[which, r], self.sibling)

    def start(self, first=0, last=None):
        for r in range(first, self.chunks if last is None else last):
            self.around(0, r).start()
            self.around(1, r).start()
            self.across(0, r).start()

    def forward(self, r):
        for way in range(2):
            self.arrived(way, r).wait_recv()
            self.onward(way, r).start()
            self.across(1 + way, r).start()

    def forward_far(self, r):
        for way in range(2):
            self.far_arrived(way, r).wait_recv()
            self.across(3 + way, r).start()

    def complete(self, r):
        for which in range(5):
            self.across(which, r, arriving=True).wait_recv()

    def sent(self):
        for r in range(self.chunks):
            for way in range(2):
                self.around(way, r).wait_send()
                self.onward(way, r).wait_send()
            for which in range(5):
                self.across(which, r).wait_send()


def gather_sems(chunks):
    dma = pltpu.SemaphoreType.DMA
    return [dma((2, chunks)), dma((2, chunks)), dma((2, chunks)), dma((2, chunks)), dma((5, chunks)), dma((5, chunks))]


def pick(index, options):
    value = options[-1]
    for i in range(len(options) - 2, -1, -1):
        value = jnp.where(index == i, options[i], value)
    return value


CHUNKS = 3
STEP = TOK // CHUNKS
PARTS_W = 4
UNITS = [
    (0, 0), (1, 0), (2, 0), (1, 1), (2, 1), (1, 2), (2, 2), (0, 1),
    (3, 0), (3, 1), (3, 2), (3, 3), (1, 3), (2, 3), (0, 2), (0, 3),
]


def attend_kernel(
    tokens, gain, w_query, w_key, w_value, w_out, w_up, att, w_full, base,
    xb, weights, turned, up_in, gains, qb, kb, vb, acc, top, o_send, l_send, o_recv, l_recv,
    local, q_ss, q_rs, k_ss, k_rs, v_ss, v_rs, far_ss, far_rs, o_ss, o_rs, l_ss, l_rs, *sems,
):
    x, y, z, core = coords()
    tok_ring = Gather(tokens, xb, TOK, CHUNKS, *sems[:6], wide=D // PARTS)
    ring = Gather(w_out, w_full, 256, PARTS_W, *sems[6:])

    def along(axis, by):
        if axis == 0:
            return device((x + by + 4) % 4, y, z, core)
        return device(x, y, (z + by + 4) % 4, core)

    offsets = {1: 1, 2: -1, 3: 2}

    def move(kind, h, slot, r):
        target = along(1 - h if kind == "q" else h, -offsets[slot])
        part = pl.ds(r * STEP, STEP)
        if kind == "q":
            src, dst, ss, rs = qb.at[h, 0, :, part], qb.at[h, slot, :, part], q_ss, q_rs
        elif kind == "k":
            src, dst, ss, rs = kb.at[h, 0, part], kb.at[h, slot, part], k_ss, k_rs
        else:
            src, dst, ss, rs = vb.at[h, 0, :, part], vb.at[h, slot, :, part], v_ss, v_rs
        return remote(src, dst, ss.at[h, slot, r], rs.at[h, slot, r], target)

    def send(r):
        for kind in "qkv":
            for slot in (1, 2):
                for h in range(2):
                    move(kind, h, slot, r).start()

    def relay(kind, h, slot):
        target = along(1 - h if kind == "q" else h, -offsets[slot])
        part = pl.ds((slot - 1) * (TOK // 2), TOK // 2)
        n = "qkv".index(kind)
        buf = (qb, kb, vb)[n]
        if kind == "k":
            src, dst = buf.at[h, slot, part], buf.at[h, 3, part]
        else:
            src, dst = buf.at[h, slot, :, part], buf.at[h, 3, :, part]
        return remote(src, dst, far_ss.at[n, h, slot - 1], far_rs.at[n, h, slot - 1], target)

    def lift(r):
        cut = pl.ds(r * STEP, STEP)
        base[cut, :] = jnp.dot(xb[:, cut].T, up_in[...], preferred_element_type=F32)

    own = pltpu.make_async_copy(
        tokens, xb.at[pl.ds(pl.multiple_of(tok_ring.own * (D // PARTS), 16), D // PARTS)], local.at[0]
    )
    own.start()
    loads = [pltpu.make_async_copy(w, weights.at[i], local.at[1 + i]) for i, w in enumerate((w_query, w_key, w_value))]
    for load in loads:
        load.start()
    own_w = pltpu.make_async_copy(w_out, w_full.at[ring.own], local.at[4])
    own_w.start()
    ups = [pltpu.make_async_copy(w_up.at[j], up_in.at[:, pl.ds(j * HD, HD)], local.at[5 + j]) for j in range(KMER)]
    for load in ups:
        load.start()
    greet([along(a, by) for a in range(2) for by in (1, -1, 2)] + ring.partners())
    tok_ring.start(0, 1)
    for i in range(D // HD):
        gains[pl.ds(i * HD, HD), :] = jnp.broadcast_to(gain[pl.ds(i, 1), :], (HD, HD)).T

    def turn(i):
        loads[i].wait()
        for j in range(D // 256):
            turned[pl.ds(i * 256, 256), pl.ds(j * 256, 256)] = weights[i, pl.ds(j * 256, 256), :].T

    scale = math.log2(math.e) / math.sqrt(HD)

    def heads(r):
        tok_ring.complete(r)
        cut = pl.ds(r * STEP, STEP)
        wide = xb[:, cut].astype(F32)
        centred = wide - jnp.mean(wide, axis=0, keepdims=True)
        variance = jnp.mean(centred * centred, axis=0, keepdims=True)
        column = jnp.concatenate([gains[...]] * (STEP // HD), axis=1)
        normed = (centred * lax.rsqrt(variance + 1e-05) * column).astype(BF16)
        qkv = jnp.dot(turned[...], normed, preferred_element_type=F32)
        for h in range(2):
            at = h * HD
            qb[h, 0, :, cut] = (qkv[at : at + HD] * scale).astype(BF16)
            kb[h, 0, cut, :] = qkv[256 + at : 256 + at + HD].T.astype(BF16)
            vb[h, 0, :, cut] = qkv[512 + at : 512 + at + HD].astype(BF16)
        send(r)

    turn(0)
    tok_ring.start(1, 2)
    turn(1)
    turn(2)
    own.wait()
    tok_ring.forward(0)
    tok_ring.start(2, 3)
    top[...] = jnp.full(top.shape, -1e30, F32)
    acc[...] = jnp.zeros(acc.shape, F32)
    tok_ring.forward(1)
    tok_ring.forward_far(0)
    heads(0)
    tok_ring.forward(2)
    tok_ring.forward_far(1)
    ring.start()
    heads(1)
    tok_ring.forward_far(2)
    heads(2)

    ones = jnp.ones((16, TOK), BF16)

    def partial(h, a):
        total = acc[h, a, HD : HD + 8, :]
        return acc[h, a, :HD, :] / total[:1], top[h, a] + jnp.log2(total)

    def give(h, slot):
        by = pick(slot - 1, [1, -1, 2])
        target = along(1 - h, by)
        return [
            remote(o_send.at[h, slot - 1], o_recv.at[h, slot - 1], o_ss.at[h, slot - 1], o_rs.at[h, slot - 1], target),
            remote(l_send.at[h, slot - 1], l_recv.at[h, slot - 1], l_ss.at[h, slot - 1], l_rs.at[h, slot - 1], target),
        ]

    def unit(i, carry):
        def arrivals(kinds, slot):
            for kind in kinds:
                for h in range(2):
                    for r in range(CHUNKS):
                        move(kind, h, slot, r).wait_recv()

        def arrivals(kinds, slot):
            for kind in kinds:
                for h in range(2):
                    for r in range(CHUNKS):
                        move(kind, h, slot, r).wait_recv()
                    relay(kind, h, slot).start()

        def far_arrivals(kinds):
            for kind in kinds:
                for h in range(2):
                    for slot in (1, 2):
                        relay(kind, h, slot).wait_recv()

        for index, kinds, slot in ((1, "q", 1), (2, "q", 2), (3, "kv", 1), (4, "kv", 2)):
            pl.when(i == index)(functools.partial(arrivals, kinds, slot))
        for index, kinds in ((8, "q"), (11, "kv")):
            pl.when(i == index)(functools.partial(far_arrivals, kinds))

        @pl.when(i == 1)
        def _():
            for load in ups:
                load.wait()
            lift(0)
            lift(1)

        for r, index in enumerate((2, 5, 9, 12)):
            pl.when(i == index)(functools.partial(ring.forward, r))
        a = pick(i, [u[0] for u in UNITS])
        b = pick(i, [u[1] for u in UNITS])
        scores = [
            jnp.dot(kb[h, b], qb[h, a], preferred_element_type=F32) for h in range(2)
        ]
        for h in range(2):
            s = scores[h]
            before = top[h, a]
            now = jnp.maximum(before, jnp.max(s, axis=0, keepdims=True))
            weights = jnp.exp2(s - now[:1]).astype(BF16)
            factor = jnp.exp2(before - now)
            lhs = jnp.concatenate([vb[h, b], ones], axis=0)
            added = jnp.dot(lhs, weights, preferred_element_type=F32)
            acc[h, a] = acc[h, a] * factor[:1] + added
            top[h, a] = now

        @pl.when(jnp.logical_and(i >= 11, i < 14))
        def _():
            for h in range(2):
                value, level = partial(h, a)
                o_send[h, a - 1] = value.astype(BF16)
                l_send[h, a - 1] = level
                for copy in give(h, a):
                    copy.start()

        return carry

    lax.fori_loop(0, len(UNITS), unit, 0)
    lift(CHUNKS - 1)
    for r in range(PARTS_W):
        ring.forward_far(r)
    for h in range(2):
        value, level = partial(h, 0)
        for slot in range(1, 4):
            for copy in give(h, slot):
                copy.wait_recv()
        levels = [level] + [l_recv[h, i] for i in range(3)]
        highest = functools.reduce(jnp.maximum, levels)
        shares = [jnp.exp2(one - highest) for one in levels]
        total = functools.reduce(jnp.add, shares)
        shares = [share / total for share in shares]
        value = value * shares[0][:1]
        for i in range(3):
            value = value + o_recv[h, i].astype(F32) * shares[1 + i][:1]
        att[:, pl.ds(h * HD, HD)] = value.T.astype(BF16)
    own_w.wait()
    for r in range(PARTS_W):
        ring.complete(r)
    tok_ring.sent()
    ring.sent()
    for h in range(2):
        for slot in (1, 2):
            for kind in "qkv":
                for r in range(CHUNKS):
                    move(kind, h, slot, r).wait_send()
                relay(kind, h, slot).wait_send()
        for slot in range(1, 4):
            for copy in give(h, slot):
                copy.wait_send()


def attend(tokens, gain, w_query, w_key, w_value, w_out, w_up):
    dma = pltpu.SemaphoreType.DMA
    return pl.pallas_call(
        attend_kernel,
        out_shape=(
            jax.ShapeDtypeStruct((TOK, 256), BF16),
            jax.ShapeDtypeStruct((PARTS, 256, D), BF16),
            jax.ShapeDtypeStruct((TOK, KMER * HD), F32),
        ),
        in_specs=[ANY, VMEM, ANY, ANY, ANY, ANY, ANY],
        out_specs=(VMEM, ANY, VMEM),
        scratch_shapes=[
            pltpu.VMEM((D, TOK), BF16),
            pltpu.VMEM((3, D, 256), BF16),
            pltpu.VMEM((768, D), BF16),
            pltpu.VMEM((D, KMER * HD), BF16),
            pltpu.VMEM((D, HD), F32),
            pltpu.VMEM((2, 4, HD, TOK), BF16),
            pltpu.VMEM((2, 4, TOK, HD), BF16),
            pltpu.VMEM((2, 4, HD, TOK), BF16),
            pltpu.VMEM((2, 4, HD + 16, TOK), F32),
            pltpu.VMEM((2, 4, 8, TOK), F32),
            pltpu.VMEM((2, 3, HD, TOK), BF16),
            pltpu.VMEM((2, 3, 8, TOK), F32),
            pltpu.VMEM((2, 3, HD, TOK), BF16),
            pltpu.VMEM((2, 3, 8, TOK), F32),
            dma((5 + KMER,)),
            *[dma((2, 4, CHUNKS)) for _ in range(6)],
            dma((3, 2, 2)),
            dma((3, 2, 2)),
            *[dma((2, 3)) for _ in range(4)],
            *gather_sems(CHUNKS),
            *gather_sems(PARTS_W),
        ],
        compiler_params=pltpu.CompilerParams(
            collective_id=0, has_side_effects=True, vmem_limit_bytes=56 << 20
        ),
    )(tokens, gain, w_query, w_key, w_value, w_out, w_up)


def gelu(x):
    return 0.5 * x * (1.0 + jnp.tanh(math.sqrt(2.0 / math.pi) * (x + 0.044715 * x * x * x)))


def expand_kernel(att, base, w_full, w_up, out, blocks, wo_v, wu_v, base_v, joint, local, *sems):
    ring = Gather(att, blocks, TOK, CHUNKS, *sems)
    ups = [pltpu.make_async_copy(w_up.at[j], wu_v.at[:, pl.ds(j * HD, HD)], local.at[2 + j]) for j in range(KMER)]
    outs = [pltpu.make_async_copy(w_full.at[j], wo_v.at[j], local.at[8 + j]) for j in range(PARTS)]
    lifted = pltpu.make_async_copy(base, base_v, local.at[1])
    own = pltpu.make_async_copy(att, blocks.at[ring.own], local.at[0])
    for load in [*ups, *outs, own, lifted]:
        load.start()
    greet(ring.partners())
    ring.start(0, 1)
    for load in ups:
        load.wait()

    def merge(i):
        outs[i].wait()
        joint[pl.ds(i * 256, 256), :] = jnp.dot(wo_v[i], wu_v[...], preferred_element_type=F32).astype(BF16)

    def finish(r):
        ring.complete(r)
        cut = pl.ds(r * STEP, STEP)
        joined = jnp.concatenate([blocks[j, cut, :] for j in range(PARTS)], axis=1)
        raised = base_v[cut, :] + jnp.dot(joined, joint[...], preferred_element_type=F32)
        out[cut, :] = gelu(raised).astype(BF16)

    merge(0)
    merge(1)
    ring.start(1, 2)
    merge(2)
    merge(3)
    ring.forward(0)
    merge(4)
    ring.start(2, 3)
    merge(5)
    merge(6)
    ring.forward(1)
    ring.forward_far(0)
    merge(7)
    own.wait()
    lifted.wait()
    ring.forward(2)
    ring.forward_far(1)
    finish(0)
    ring.forward_far(2)
    finish(1)
    finish(2)
    ring.sent()


def expand(att, base, w_full, w_up):
    return pl.pallas_call(
        expand_kernel,
        out_shape=jax.ShapeDtypeStruct((TOK, KMER * HD), BF16),
        in_specs=[ANY] * 4,
        out_specs=VMEM,
        scratch_shapes=[
            pltpu.VMEM((PARTS, TOK, 256), BF16),
            pltpu.VMEM((PARTS, 256, D), BF16),
            pltpu.VMEM((D, KMER * HD), BF16),
            pltpu.VMEM((TOK, KMER * HD), F32),
            pltpu.VMEM((PARTS * 256, KMER * HD), BF16),
            pltpu.SemaphoreType.DMA((16,)),
            *gather_sems(CHUNKS),
        ],
        compiler_params=pltpu.CompilerParams(
            collective_id=2, has_side_effects=True, vmem_limit_bytes=56 << 20
        ),
    )(att, base, w_full, w_up)


def place_kernel(starts, lengths, expanded, w_class, own, lead, logits, lead_logits, wide, placed, classes):
    for j in range(KMER):
        wide[pl.ds(j, TOK, stride=8), :] = expanded[:, j * HD : (j + 1) * HD].astype(F32)
    placed[:LEAD, :] = jnp.zeros((LEAD, HD), F32)
    placed[NUC:, :] = jnp.zeros((LEAD + 16, HD), F32)
    classes[...] = jnp.zeros(classes.shape, F32)
    classes[:CLASSES, :] = w_class[...].astype(F32)
    shift = LEAD - lax.axis_index("seq") * NUC

    def one(t, carry):
        placed[pl.ds(starts[t] + shift, 8), :] = wide[pl.ds(pl.multiple_of(t * 8, 8), 8), :]
        return carry

    lax.fori_loop(0, TOK, one, 0, unroll=8)
    end = starts[TOK - 1] + lengths[TOK - 1] + shift
    placed[pl.ds(end, 8), :] = jnp.zeros((8, HD), F32)
    first = placed[:LEAD, :].astype(BF16)
    lead[...] = first
    rows = placed[LEAD : LEAD + NUC, :].astype(BF16)
    own[...] = rows
    spread = classes[...].astype(BF16)
    partial = lax.dot_general(spread, rows, NT, preferred_element_type=F32).astype(BF16)
    for j in range(PARTS - 1):
        logits[j] = partial[:, j * PIECE : (j + 1) * PIECE]
    rest = NUC - (PARTS - 1) * PIECE
    logits[PARTS - 1, :, :rest] = partial[:, (PARTS - 1) * PIECE :]
    logits[PARTS - 1, :, rest:] = jnp.zeros((16, PIECE - rest), BF16)
    lead_logits[...] = lax.dot_general(spread, first, NT, preferred_element_type=F32).astype(BF16)


def place(starts, lengths, expanded, w_class):
    return pl.pallas_call(
        place_kernel,
        out_shape=(
            jax.ShapeDtypeStruct((NUC, HD), BF16),
            jax.ShapeDtypeStruct((LEAD, HD), BF16),
            jax.ShapeDtypeStruct((PARTS, 16, PIECE), BF16),
            jax.ShapeDtypeStruct((16, LEAD), BF16),
        ),
        in_specs=[SMEM, SMEM, VMEM, VMEM],
        out_specs=(VMEM, VMEM, VMEM, VMEM),
        scratch_shapes=[
            pltpu.VMEM((TOK * 8, HD), F32),
            pltpu.VMEM((LEAD + NUC + 16, HD), F32),
            pltpu.VMEM((16, HD), F32),
        ],
        compiler_params=pltpu.CompilerParams(vmem_limit_bytes=48 << 20),
    )(starts, lengths, expanded, w_class)


def loss_kernel(
    lead, pieces, lead_logits, labels, arriving, loss,
    received, early, late, total, lab, mine, lead_ss, lead_rs, p_ss, p_rs, e_ss, e_rs, t_ss, t_rs, a_ss, a_rs, lab_sem,
):
    seq = lax.axis_index("seq")
    mp = lax.axis_index("mp")
    before, after = (seq + 15) % 16, (seq + 1) % 16
    others = [{"seq": seq, "mp": (mp + d) % PARTS} for d in range(1, PARTS)]
    head = NUC - (PARTS - 1) * PIECE
    split = (PARTS - 1) * PIECE - (NUC - LEAD)
    lab_head = pltpu.make_async_copy(
        labels.at[:, pl.ds(pl.multiple_of(mp * PIECE, PIECE), head)], lab.at[:, pl.ds(0, head)], lab_sem.at[0]
    )
    lab_tail = pltpu.make_async_copy(
        labels.at[:, pl.ds(pl.multiple_of(jnp.minimum(mp, PARTS - 2) * PIECE + head, HD), PIECE - head)],
        lab.at[:, pl.ds(head, PIECE - head)], lab_sem.at[1],
    )
    lab_head.start()
    lab_tail.start()

    barrier = pltpu.get_barrier_semaphore()
    for other in others + [{"seq": after, "mp": mp}]:
        pl.semaphore_signal(barrier, inc=1, device_id=other, device_id_type=MESH)

    @pl.when(mp >= PARTS - 2)
    def _():
        for j in range(PARTS):
            pl.semaphore_signal(barrier, inc=1, device_id={"seq": after, "mp": j}, device_id_type=MESH)

    pl.semaphore_wait(barrier, PARTS + 2)

    def piece(d):
        return remote(
            pieces.at[(mp + d) % PARTS], received.at[d - 1], p_ss.at[d - 1], p_rs.at[d - 1], others[d - 1]
        )

    def early_copy(slot):
        return remote(
            lead_logits.at[:, pl.ds(0, split)], early.at[slot], e_ss, e_rs.at[slot], {"seq": before, "mp": PARTS - 2}
        )

    def late_copy(slot):
        return remote(
            lead_logits.at[:, pl.ds(split, head)], late.at[slot], t_ss, t_rs.at[slot], {"seq": before, "mp": PARTS - 1}
        )

    early_copy(mp).start()
    late_copy(mp).start()
    for d in range(1, PARTS):
        piece(d).start()
    shift = remote(lead, arriving, lead_ss, lead_rs, {"seq": before, "mp": mp})
    lab_head.wait()
    lab_tail.wait()
    for d in range(1, PARTS):
        piece(d).wait_recv()
    shift.start()
    summed = pieces[mp].astype(F32)
    for d in range(1, PARTS):
        summed = summed + received[d - 1].astype(F32)
    total[...] = summed

    @pl.when(mp == PARTS - 2)
    def _():
        for j in range(PARTS):
            early_copy(j).wait_recv()
        for j in range(PARTS):
            total[:, PIECE - split :] = total[:, PIECE - split :] + early[j].astype(F32)

    @pl.when(mp == PARTS - 1)
    def _():
        for j in range(PARTS):
            late_copy(j).wait_recv()
        for j in range(PARTS):
            total[:, :head] = total[:, :head] + late[j].astype(F32)

    logit = total[:CLASSES, :]
    softplus = jnp.maximum(logit, 0.0) + jnp.log(1.0 + jnp.exp(-jnp.abs(logit)))
    terms = softplus - lab[...].astype(F32) * logit
    mine[...] = jnp.broadcast_to(jnp.sum(terms, axis=0, keepdims=True), (8, PIECE))

    def spread(d):
        return remote(mine, loss.at[mp], a_ss.at[d - 1], a_rs.at[d - 1], others[d - 1])

    for d in range(1, PARTS):
        spread(d).start()
    loss[mp] = mine[...]
    for d in range(1, PARTS):
        spread(d).wait_recv()
    shift.wait()
    early_copy(mp).wait_send()
    late_copy(mp).wait_send()
    for d in range(1, PARTS):
        piece(d).wait_send()
        spread(d).wait_send()


def losses(lead, pieces, lead_logits, labels):
    dma = pltpu.SemaphoreType.DMA
    head = NUC - (PARTS - 1) * PIECE
    return pl.pallas_call(
        loss_kernel,
        out_shape=(
            jax.ShapeDtypeStruct((LEAD, HD), BF16),
            jax.ShapeDtypeStruct((PARTS, 8, PIECE), F32),
        ),
        in_specs=[VMEM, VMEM, VMEM, ANY],
        out_specs=(VMEM, VMEM),
        scratch_shapes=[
            pltpu.VMEM((PARTS - 1, 16, PIECE), BF16),
            pltpu.VMEM((PARTS, 16, LEAD - head), BF16),
            pltpu.VMEM((PARTS, 16, head), BF16),
            pltpu.VMEM((16, PIECE), F32),
            pltpu.VMEM((CLASSES, PIECE), jnp.int32),
            pltpu.VMEM((8, PIECE), F32),
            dma, dma, dma((7,)), dma((7,)), dma, dma((PARTS,)), dma, dma((PARTS,)), dma((7,)), dma((7,)), dma((2,)),
        ],
        compiler_params=pltpu.CompilerParams(
            collective_id=3, has_side_effects=True, vmem_limit_bytes=32 << 20
        ),
    )(lead, pieces, lead_logits, labels)


def per_device(
    tokens, norm_gain, w_query, w_key, w_value, w_out, w_up, w_class, starts, lengths, labels
):
    att, w_full, base = attend(tokens.T, norm_gain.reshape(D // HD, HD), w_query, w_key, w_value, w_out, w_up)
    expanded = expand(att, base, w_full, w_up)
    own, lead, logits, lead_logits = place(starts, lengths, expanded, w_class.T)
    arriving, loss = losses(lead, logits, lead_logits, labels.T)
    features = own.at[NUC - LEAD :].add(arriving)
    return (features, loss[:, 0, :].reshape(-1)[:NUC])


def solution(mesh):
    return jax.shard_map(
        per_device,
        mesh=mesh,
        in_specs=(
            P("seq", "mp"),
            P(),
            P(None, "mp"),
            P(None, "mp"),
            P(None, "mp"),
            P("mp", None),
            P(None, None, "mp"),
            P("mp", None),
            P("seq"),
            P("seq"),
            P("seq", None),
        ),
        out_specs=(P("seq", "mp"), P("seq")),
        check_vma=False,
    )
```

```python
import functools
import math

import jax
import jax.numpy as jnp
from jax import lax
from jax.experimental import pallas as pl
from jax.experimental.pallas import tpu as pltpu
from jax.sharding import PartitionSpec as P

HD = 128
KMER = 6
TOK = 768
D = 2560
NUC = 3968
LEAD = 640
PIECE = 512
PARTS = 8
CLASSES = 14
MESH = pl.DeviceIdType.MESH
ANY = pl.BlockSpec(memory_space=pl.ANY)
VMEM = pl.BlockSpec(memory_space=pltpu.VMEM)
SMEM = pl.BlockSpec(memory_space=pltpu.SMEM)
BF16 = jnp.bfloat16
F32 = jnp.float32
NT = (((1,), (1,)), ((), ()))


def coords():
    seq = lax.axis_index("seq")
    mp = lax.axis_index("mp")
    return seq // 4, mp // 2, seq % 4, mp % 2


def device(x, y, z, core):
    return {"seq": x * 4 + z, "mp": y * 2 + core}


def greet(partners):
    barrier = pltpu.get_barrier_semaphore()
    for partner in partners:
        pl.semaphore_signal(barrier, inc=1, device_id=partner, device_id_type=MESH)
    pl.semaphore_wait(barrier, len(partners))


def remote(src, dst, send_sem, recv_sem, target):
    return pltpu.make_async_remote_copy(
        src_ref=src, dst_ref=dst, send_sem=send_sem, recv_sem=recv_sem, device_id=target, device_id_type=MESH
    )


class Gather:
    def __init__(self, src, buf, extent, chunks, y_send, y_recv, f_send, f_recv, c_send, c_recv, wide=0):
        self.src, self.buf, self.step, self.wide = src, buf, extent // chunks, wide
        self.chunks = chunks
        self.sems = (y_send, y_recv, f_send, f_recv, c_send, c_recv)
        x, y, z, core = coords()
        up, down, far = (y + 1) % 4, (y + 3) % 4, (y + 2) % 4
        self.up, self.down = device(x, up, z, core), device(x, down, z, core)
        self.sibling = device(x, y, z, 1 - core)
        self.own = y * 2 + core
        self.slots = [y * 2 + core, down * 2 + core, up * 2 + core, far * 2 + core]
        self.twins = [y * 2 + 1 - core, down * 2 + 1 - core, up * 2 + 1 - core, far * 2 + 1 - core]

    def partners(self):
        return [self.up, self.down, self.sibling]

    def cut(self, r, part):
        if part is None:
            return pl.ds(r * self.step, self.step)
        half = self.step // 2
        return pl.ds(r * self.step + part * half, half)

    def mine(self, r):
        cut = self.cut(r, None)
        return self.src.at[:, cut] if self.wide else self.src.at[cut]

    def at(self, slot, r, part=None):
        cut = self.cut(r, part)
        if self.wide:
            return self.buf.at[pl.ds(pl.multiple_of(slot * self.wide, 16), self.wide), cut]
        return self.buf.at[slot, cut]

    def toward(self, way):
        return self.up if way == 0 else self.down

    def around(self, way, r):
        y_send, y_recv = self.sems[:2]
        return remote(self.mine(r), self.at(self.own, r), y_send.at[way, r], y_recv.at[way, r], self.toward(way))

    def arrived(self, way, r):
        y_send, y_recv = self.sems[:2]
        slot = self.at(self.slots[1 + way], r)
        return remote(slot, slot, y_send.at[way, r], y_recv.at[way, r], self.toward(way))

    def onward(self, way, r):
        f_send, f_recv = self.sems[2:4]
        slot = self.at(self.slots[1 + way], r, way)
        return remote(slot, slot, f_send.at[way, r], f_recv.at[way, r], self.toward(way))

    def far_arrived(self, way, r):
        f_send, f_recv = self.sems[2:4]
        slot = self.at(self.slots[3], r, way)
        return remote(slot, slot, f_send.at[way, r], f_recv.at[way, r], self.toward(way))

    def across(self, which, r, arriving=False):
        c_send, c_recv = self.sems[4:]
        part = which - 3 if which >= 3 else None
        slots = self.twins if arriving else self.slots
        slot = self.at(slots[min(which, 3)], r, part)
        src = self.mine(r) if which == 0 and not arriving else slot
        return remote(src, slot, c_send.at[which, r], c_recv.at[which, r], self.sibling)

    def start(self, first=0, last=None):
        for r in range(first, self.chunks if last is None else last):
            self.around(0, r).start()
            self.around(1, r).start()
            self.across(0, r).start()

    def forward(self, r):
        for way in range(2):
            self.arrived(way, r).wait_recv()
            self.onward(way, r).start()
            self.across(1 + way, r).start()

    def forward_far(self, r):
        for way in range(2):
            self.far_arrived(way, r).wait_recv()
            self.across(3 + way, r).start()

    def complete(self, r):
        for which in range(5):
            self.across(which, r, arriving=True).wait_recv()

    def sent(self):
        for r in range(self.chunks):
            for way in range(2):
                self.around(way, r).wait_send()
                self.onward(way, r).wait_send()
            for which in range(5):
                self.across(which, r).wait_send()


def gather_sems(chunks):
    dma = pltpu.SemaphoreType.DMA
    return [dma((2, chunks)), dma((2, chunks)), dma((2, chunks)), dma((2, chunks)), dma((5, chunks)), dma((5, chunks))]


def pick(index, options):
    value = options[-1]
    for i in range(len(options) - 2, -1, -1):
        value = jnp.where(index == i, options[i], value)
    return value


CHUNKS = 3
STEP = TOK // CHUNKS
PARTS_W = 4
UNITS = [
    (0, 0), (1, 0), (2, 0), (1, 1), (2, 1), (1, 2), (2, 2), (0, 1),
    (3, 0), (3, 1), (3, 2), (3, 3), (1, 3), (2, 3), (0, 2), (0, 3),
]


def attend_kernel(
    tokens, gain, w_query, w_key, w_value, w_out, w_up, att, w_full, base,
    xb, weights, turned, up_in, gains, qb, kb, vb, acc, top, o_send, l_send, o_recv, l_recv,
    local, q_ss, q_rs, k_ss, k_rs, v_ss, v_rs, far_ss, far_rs, o_ss, o_rs, l_ss, l_rs, *sems,
):
    x, y, z, core = coords()
    tok_ring = Gather(tokens, xb, TOK, CHUNKS, *sems[:6], wide=D // PARTS)
    ring = Gather(w_out, w_full, 256, PARTS_W, *sems[6:])

    def along(axis, by):
        if axis == 0:
            return device((x + by + 4) % 4, y, z, core)
        return device(x, y, (z + by + 4) % 4, core)

    offsets = {1: 1, 2: -1, 3: 2}

    def move(kind, h, slot, r):
        target = along(1 - h if kind == "q" else h, -offsets[slot])
        part = pl.ds(r * STEP, STEP)
        if kind == "q":
            src, dst, ss, rs = qb.at[h, 0, :, part], qb.at[h, slot, :, part], q_ss, q_rs
        elif kind == "k":
            src, dst, ss, rs = kb.at[h, 0, part], kb.at[h, slot, part], k_ss, k_rs
        else:
            src, dst, ss, rs = vb.at[h, 0, :, part], vb.at[h, slot, :, part], v_ss, v_rs
        return remote(src, dst, ss.at[h, slot, r], rs.at[h, slot, r], target)

    def send(r):
        for kind in "qkv":
            for slot in (1, 2):
                for h in range(2):
                    move(kind, h, slot, r).start()

    def relay(kind, h, slot):
        target = along(1 - h if kind == "q" else h, -offsets[slot])
        part = pl.ds((slot - 1) * (TOK // 2), TOK // 2)
        n = "qkv".index(kind)
        buf = (qb, kb, vb)[n]
        if kind == "k":
            src, dst = buf.at[h, slot, part], buf.at[h, 3, part]
        else:
            src, dst = buf.at[h, slot, :, part], buf.at[h, 3, :, part]
        return remote(src, dst, far_ss.at[n, h, slot - 1], far_rs.at[n, h, slot - 1], target)

    def lift(r):
        cut = pl.ds(r * STEP, STEP)
        base[cut, :] = jnp.dot(xb[:, cut].T, up_in[...], preferred_element_type=F32)

    own = pltpu.make_async_copy(
        tokens, xb.at[pl.ds(pl.multiple_of(tok_ring.own * (D // PARTS), 16), D // PARTS)], local.at[0]
    )
    own.start()
    loads = [pltpu.make_async_copy(w, weights.at[i], local.at[1 + i]) for i, w in enumerate((w_query, w_key, w_value))]
    for load in loads:
        load.start()
    own_w = pltpu.make_async_copy(w_out, w_full.at[ring.own], local.at[4])
    own_w.start()
    ups = [pltpu.make_async_copy(w_up.at[j], up_in.at[:, pl.ds(j * HD, HD)], local.at[5 + j]) for j in range(KMER)]
    for load in ups:
        load.start()
    greet([along(a, by) for a in range(2) for by in (1, -1, 2)] + ring.partners())
    tok_ring.start(0, 1)
    for i in range(D // HD):
        gains[pl.ds(i * HD, HD), :] = jnp.broadcast_to(gain[pl.ds(i, 1), :], (HD, HD)).T

    def turn(i):
        loads[i].wait()
        for j in range(D // 256):
            turned[pl.ds(i * 256, 256), pl.ds(j * 256, 256)] = weights[i, pl.ds(j * 256, 256), :].T

    scale = math.log2(math.e) / math.sqrt(HD)

    def heads(r):
        tok_ring.complete(r)
        cut = pl.ds(r * STEP, STEP)
        wide = xb[:, cut].astype(F32)
        centred = wide - jnp.mean(wide, axis=0, keepdims=True)
        variance = jnp.mean(centred * centred, axis=0, keepdims=True)
        column = jnp.concatenate([gains[...]] * (STEP // HD), axis=1)
        normed = (centred * lax.rsqrt(variance + 1e-05) * column).astype(BF16)
        qkv = jnp.dot(turned[...], normed, preferred_element_type=F32)
        for h in range(2):
            at = h * HD
            qb[h, 0, :, cut] = (qkv[at : at + HD] * scale).astype(BF16)
            kb[h, 0, cut, :] = qkv[256 + at : 256 + at + HD].T.astype(BF16)
            vb[h, 0, :, cut] = qkv[512 + at : 512 + at + HD].astype(BF16)
        send(r)

    turn(0)
    tok_ring.start(1, 2)
    turn(1)
    turn(2)
    own.wait()
    tok_ring.forward(0)
    tok_ring.start(2, 3)
    top[...] = jnp.full(top.shape, -1e30, F32)
    acc[...] = jnp.zeros(acc.shape, F32)
    tok_ring.forward(1)
    tok_ring.forward_far(0)
    heads(0)
    tok_ring.forward(2)
    tok_ring.forward_far(1)
    ring.start()
    heads(1)
    tok_ring.forward_far(2)
    heads(2)

    ones = jnp.ones((16, TOK), BF16)

    def partial(h, a):
        total = acc[h, a, HD : HD + 8, :]
        return acc[h, a, :HD, :] / total[:1], top[h, a] + jnp.log2(total)

    def give(h, slot):
        by = pick(slot - 1, [1, -1, 2])
        target = along(1 - h, by)
        return [
            remote(o_send.at[h, slot - 1], o_recv.at[h, slot - 1], o_ss.at[h, slot - 1], o_rs.at[h, slot - 1], target),
            remote(l_send.at[h, slot - 1], l_recv.at[h, slot - 1], l_ss.at[h, slot - 1], l_rs.at[h, slot - 1], target),
        ]

    def unit(i, carry):
        def arrivals(kinds, slot):
            for kind in kinds:
                for h in range(2):
                    for r in range(CHUNKS):
                        move(kind, h, slot, r).wait_recv()

        def arrivals(kinds, slot):
            for kind in kinds:
                for h in range(2):
                    for r in range(CHUNKS):
                        move(kind, h, slot, r).wait_recv()
                    relay(kind, h, slot).start()

        def far_arrivals(kinds):
            for kind in kinds:
                for h in range(2):
                    for slot in (1, 2):
                        relay(kind, h, slot).wait_recv()

        for index, kinds, slot in ((1, "q", 1), (2, "q", 2), (3, "kv", 1), (4, "kv", 2)):
            pl.when(i == index)(functools.partial(arrivals, kinds, slot))
        for index, kinds in ((8, "q"), (11, "kv")):
            pl.when(i == index)(functools.partial(far_arrivals, kinds))

        @pl.when(i == 1)
        def _():
            for load in ups:
                load.wait()
            lift(0)
            lift(1)

        for r, index in enumerate((2, 5, 9, 12)):
            pl.when(i == index)(functools.partial(ring.forward, r))
        a = pick(i, [u[0] for u in UNITS])
        b = pick(i, [u[1] for u in UNITS])
        scores = [
            jnp.dot(kb[h, b], qb[h, a], preferred_element_type=F32) for h in range(2)
        ]
        for h in range(2):
            s = scores[h]
            before = top[h, a]
            now = jnp.maximum(before, jnp.max(s, axis=0, keepdims=True))
            weights = jnp.exp2(s - now[:1]).astype(BF16)
            factor = jnp.exp2(before - now)
            lhs = jnp.concatenate([vb[h, b], ones], axis=0)
            added = jnp.dot(lhs, weights, preferred_element_type=F32)
            acc[h, a] = acc[h, a] * factor[:1] + added
            top[h, a] = now

        @pl.when(jnp.logical_and(i >= 11, i < 14))
        def _():
            for h in range(2):
                value, level = partial(h, a)
                o_send[h, a - 1] = value.astype(BF16)
                l_send[h, a - 1] = level
                for copy in give(h, a):
                    copy.start()

        return carry

    lax.fori_loop(0, len(UNITS), unit, 0)
    lift(CHUNKS - 1)
    for r in range(PARTS_W):
        ring.forward_far(r)
    for h in range(2):
        value, level = partial(h, 0)
        for slot in range(1, 4):
            for copy in give(h, slot):
                copy.wait_recv()
        levels = [level] + [l_recv[h, i] for i in range(3)]
        highest = functools.reduce(jnp.maximum, levels)
        shares = [jnp.exp2(one - highest) for one in levels]
        total = functools.reduce(jnp.add, shares)
        shares = [share / total for share in shares]
        value = value * shares[0][:1]
        for i in range(3):
            value = value + o_recv[h, i].astype(F32) * shares[1 + i][:1]
        att[:, pl.ds(h * HD, HD)] = value.T.astype(BF16)
    own_w.wait()
    for r in range(PARTS_W):
        ring.complete(r)
    tok_ring.sent()
    ring.sent()
    for h in range(2):
        for slot in (1, 2):
            for kind in "qkv":
                for r in range(CHUNKS):
                    move(kind, h, slot, r).wait_send()
                relay(kind, h, slot).wait_send()
        for slot in range(1, 4):
            for copy in give(h, slot):
                copy.wait_send()


def attend(tokens, gain, w_query, w_key, w_value, w_out, w_up):
    dma = pltpu.SemaphoreType.DMA
    return pl.pallas_call(
        attend_kernel,
        out_shape=(
            jax.ShapeDtypeStruct((TOK, 256), BF16),
            jax.ShapeDtypeStruct((PARTS, 256, D), BF16),
            jax.ShapeDtypeStruct((TOK, KMER * HD), F32),
        ),
        in_specs=[ANY, VMEM, ANY, ANY, ANY, ANY, ANY],
        out_specs=(VMEM, ANY, VMEM),
        scratch_shapes=[
            pltpu.VMEM((D, TOK), BF16),
            pltpu.VMEM((3, D, 256), BF16),
            pltpu.VMEM((768, D), BF16),
            pltpu.VMEM((D, KMER * HD), BF16),
            pltpu.VMEM((D, HD), F32),
            pltpu.VMEM((2, 4, HD, TOK), BF16),
            pltpu.VMEM((2, 4, TOK, HD), BF16),
            pltpu.VMEM((2, 4, HD, TOK), BF16),
            pltpu.VMEM((2, 4, HD + 16, TOK), F32),
            pltpu.VMEM((2, 4, 8, TOK), F32),
            pltpu.VMEM((2, 3, HD, TOK), BF16),
            pltpu.VMEM((2, 3, 8, TOK), F32),
            pltpu.VMEM((2, 3, HD, TOK), BF16),
            pltpu.VMEM((2, 3, 8, TOK), F32),
            dma((5 + KMER,)),
            *[dma((2, 4, CHUNKS)) for _ in range(6)],
            dma((3, 2, 2)),
            dma((3, 2, 2)),
            *[dma((2, 3)) for _ in range(4)],
            *gather_sems(CHUNKS),
            *gather_sems(PARTS_W),
        ],
        compiler_params=pltpu.CompilerParams(
            collective_id=0, has_side_effects=True, vmem_limit_bytes=56 << 20
        ),
    )(tokens, gain, w_query, w_key, w_value, w_out, w_up)


def gelu(x):
    return 0.5 * x * (1.0 + jnp.tanh(math.sqrt(2.0 / math.pi) * (x + 0.044715 * x * x * x)))


def expand_kernel(att, base, w_full, w_up, out, blocks, wo_v, wu_v, base_v, joint, local, *sems):
    ring = Gather(att, blocks, TOK, CHUNKS, *sems)
    ups = [pltpu.make_async_copy(w_up.at[j], wu_v.at[:, pl.ds(j * HD, HD)], local.at[2 + j]) for j in range(KMER)]
    outs = [pltpu.make_async_copy(w_full.at[j], wo_v.at[j], local.at[8 + j]) for j in range(PARTS)]
    lifted = pltpu.make_async_copy(base, base_v, local.at[1])
    own = pltpu.make_async_copy(att, blocks.at[ring.own], local.at[0])
    for load in [*ups, *outs, own, lifted]:
        load.start()
    greet(ring.partners())
    ring.start(0, 1)
    for load in ups:
        load.wait()

    def merge(i):
        outs[i].wait()
        joint[pl.ds(i * 256, 256), :] = jnp.dot(wo_v[i], wu_v[...], preferred_element_type=F32).astype(BF16)

    def finish(r):
        ring.complete(r)
        cut = pl.ds(r * STEP, STEP)
        joined = jnp.concatenate([blocks[j, cut, :] for j in range(PARTS)], axis=1)
        raised = base_v[cut, :] + jnp.dot(joined, joint[...], preferred_element_type=F32)
        out[cut, :] = gelu(raised).astype(BF16)

    merge(0)
    merge(1)
    ring.start(1, 2)
    merge(2)
    merge(3)
    ring.forward(0)
    merge(4)
    ring.start(2, 3)
    merge(5)
    merge(6)
    ring.forward(1)
    ring.forward_far(0)
    merge(7)
    own.wait()
    lifted.wait()
    ring.forward(2)
    ring.forward_far(1)
    finish(0)
    ring.forward_far(2)
    finish(1)
    finish(2)
    ring.sent()


def expand(att, base, w_full, w_up):
    return pl.pallas_call(
        expand_kernel,
        out_shape=jax.ShapeDtypeStruct((TOK, KMER * HD), BF16),
        in_specs=[ANY] * 4,
        out_specs=VMEM,
        scratch_shapes=[
            pltpu.VMEM((PARTS, TOK, 256), BF16),
            pltpu.VMEM((PARTS, 256, D), BF16),
            pltpu.VMEM((D, KMER * HD), BF16),
            pltpu.VMEM((TOK, KMER * HD), F32),
            pltpu.VMEM((PARTS * 256, KMER * HD), BF16),
            pltpu.SemaphoreType.DMA((16,)),
            *gather_sems(CHUNKS),
        ],
        compiler_params=pltpu.CompilerParams(
            collective_id=2, has_side_effects=True, vmem_limit_bytes=56 << 20
        ),
    )(att, base, w_full, w_up)


def place_kernel(starts, lengths, expanded, w_class, own, lead, logits, lead_logits, wide, placed, classes, part, sems):
    loads = [
        pltpu.make_async_copy(expanded.at[:, pl.ds(j * HD, HD)], part.at[j], sems.at[j]) for j in range(KMER)
    ]
    for load in loads:
        load.start()
    placed[:LEAD, :] = jnp.zeros((LEAD, HD), F32)
    placed[NUC:, :] = jnp.zeros((LEAD + 16, HD), F32)
    classes[...] = jnp.zeros(classes.shape, F32)
    classes[:CLASSES, :] = w_class[...].astype(F32)
    shift = LEAD - lax.axis_index("seq") * NUC
    for j in range(KMER):
        loads[j].wait()
        wide[pl.ds(j, TOK, stride=8), :] = part[j].astype(F32)

    def one(t, carry):
        placed[pl.ds(starts[t] + shift, 8), :] = wide[pl.ds(pl.multiple_of(t * 8, 8), 8), :]
        return carry

    lax.fori_loop(0, TOK, one, 0, unroll=8)
    end = starts[TOK - 1] + lengths[TOK - 1] + shift
    placed[pl.ds(end, 8), :] = jnp.zeros((8, HD), F32)
    first = placed[:LEAD, :].astype(BF16)
    lead[...] = first
    rows = placed[LEAD : LEAD + NUC, :].astype(BF16)
    own[...] = rows
    spread = classes[...].astype(BF16)
    partial = lax.dot_general(spread, rows, NT, preferred_element_type=F32).astype(BF16)
    for j in range(PARTS - 1):
        logits[j] = partial[:, j * PIECE : (j + 1) * PIECE]
    rest = NUC - (PARTS - 1) * PIECE
    logits[PARTS - 1, :, :rest] = partial[:, (PARTS - 1) * PIECE :]
    logits[PARTS - 1, :, rest:] = jnp.zeros((16, PIECE - rest), BF16)
    lead_logits[...] = lax.dot_general(spread, first, NT, preferred_element_type=F32).astype(BF16)


def place(starts, lengths, expanded, w_class):
    return pl.pallas_call(
        place_kernel,
        out_shape=(
            jax.ShapeDtypeStruct((NUC, HD), BF16),
            jax.ShapeDtypeStruct((LEAD, HD), BF16),
            jax.ShapeDtypeStruct((PARTS, 16, PIECE), BF16),
            jax.ShapeDtypeStruct((16, LEAD), BF16),
        ),
        in_specs=[SMEM, SMEM, ANY, VMEM],
        out_specs=(VMEM, VMEM, VMEM, VMEM),
        scratch_shapes=[
            pltpu.VMEM((TOK * 8, HD), F32),
            pltpu.VMEM((LEAD + NUC + 16, HD), F32),
            pltpu.VMEM((16, HD), F32),
            pltpu.VMEM((KMER, TOK, HD), BF16),
            pltpu.SemaphoreType.DMA((KMER,)),
        ],
        compiler_params=pltpu.CompilerParams(vmem_limit_bytes=48 << 20),
    )(starts, lengths, expanded, w_class)


def loss_kernel(
    lead, pieces, lead_logits, labels, arriving, loss,
    received, early, late, total, lab, mine, lead_ss, lead_rs, p_ss, p_rs, e_ss, e_rs, t_ss, t_rs, a_ss, a_rs, lab_sem,
):
    seq = lax.axis_index("seq")
    mp = lax.axis_index("mp")
    before, after = (seq + 15) % 16, (seq + 1) % 16
    others = [{"seq": seq, "mp": (mp + d) % PARTS} for d in range(1, PARTS)]
    head = NUC - (PARTS - 1) * PIECE
    split = (PARTS - 1) * PIECE - (NUC - LEAD)
    lab_head = pltpu.make_async_copy(
        labels.at[:, pl.ds(pl.multiple_of(mp * PIECE, PIECE), head)], lab.at[:, pl.ds(0, head)], lab_sem.at[0]
    )
    lab_tail = pltpu.make_async_copy(
        labels.at[:, pl.ds(pl.multiple_of(jnp.minimum(mp, PARTS - 2) * PIECE + head, HD), PIECE - head)],
        lab.at[:, pl.ds(head, PIECE - head)], lab_sem.at[1],
    )
    lab_head.start()
    lab_tail.start()

    barrier = pltpu.get_barrier_semaphore()
    for other in others + [{"seq": after, "mp": mp}]:
        pl.semaphore_signal(barrier, inc=1, device_id=other, device_id_type=MESH)

    @pl.when(mp >= PARTS - 2)
    def _():
        for j in range(PARTS):
            pl.semaphore_signal(barrier, inc=1, device_id={"seq": after, "mp": j}, device_id_type=MESH)

    pl.semaphore_wait(barrier, PARTS + 2)

    def piece(d):
        return remote(
            pieces.at[(mp + d) % PARTS], received.at[d - 1], p_ss.at[d - 1], p_rs.at[d - 1], others[d - 1]
        )

    def early_copy(slot):
        return remote(
            lead_logits.at[:, pl.ds(0, split)], early.at[slot], e_ss, e_rs.at[slot], {"seq": before, "mp": PARTS - 2}
        )

    def late_copy(slot):
        return remote(
            lead_logits.at[:, pl.ds(split, head)], late.at[slot], t_ss, t_rs.at[slot], {"seq": before, "mp": PARTS - 1}
        )

    early_copy(mp).start()
    late_copy(mp).start()
    for d in range(1, PARTS):
        piece(d).start()
    shifts = []
    for i in range(2):
        part = pl.ds(i * (LEAD // 2), LEAD // 2)
        shifts.append(
            remote(lead.at[part], arriving.at[part], lead_ss.at[i], lead_rs.at[i], {"seq": before, "mp": mp})
        )
    shifts[0].start()
    lab_head.wait()
    lab_tail.wait()
    for d in range(1, PARTS):
        piece(d).wait_recv()
    shifts[1].start()
    summed = pieces[mp].astype(F32)
    for d in range(1, PARTS):
        summed = summed + received[d - 1].astype(F32)
    total[...] = summed

    @pl.when(mp == PARTS - 2)
    def _():
        for j in range(PARTS):
            early_copy(j).wait_recv()
        for j in range(PARTS):
            total[:, PIECE - split :] = total[:, PIECE - split :] + early[j].astype(F32)

    @pl.when(mp == PARTS - 1)
    def _():
        for j in range(PARTS):
            late_copy(j).wait_recv()
        for j in range(PARTS):
            total[:, :head] = total[:, :head] + late[j].astype(F32)

    logit = total[:CLASSES, :]
    softplus = jnp.maximum(logit, 0.0) + jnp.log(1.0 + jnp.exp(-jnp.abs(logit)))
    terms = softplus - lab[...].astype(F32) * logit
    mine[...] = jnp.broadcast_to(jnp.sum(terms, axis=0, keepdims=True), (8, PIECE))

    def spread(d):
        return remote(mine, loss.at[mp], a_ss.at[d - 1], a_rs.at[d - 1], others[d - 1])

    for d in range(1, PARTS):
        spread(d).start()
    loss[mp] = mine[...]
    for d in range(1, PARTS):
        spread(d).wait_recv()
    for shift in shifts:
        shift.wait()
    early_copy(mp).wait_send()
    late_copy(mp).wait_send()
    for d in range(1, PARTS):
        piece(d).wait_send()
        spread(d).wait_send()


def losses(lead, pieces, lead_logits, labels):
    dma = pltpu.SemaphoreType.DMA
    head = NUC - (PARTS - 1) * PIECE
    return pl.pallas_call(
        loss_kernel,
        out_shape=(
            jax.ShapeDtypeStruct((LEAD, HD), BF16),
            jax.ShapeDtypeStruct((PARTS, 8, PIECE), F32),
        ),
        in_specs=[VMEM, VMEM, VMEM, ANY],
        out_specs=(VMEM, VMEM),
        scratch_shapes=[
            pltpu.VMEM((PARTS - 1, 16, PIECE), BF16),
            pltpu.VMEM((PARTS, 16, LEAD - head), BF16),
            pltpu.VMEM((PARTS, 16, head), BF16),
            pltpu.VMEM((16, PIECE), F32),
            pltpu.VMEM((CLASSES, PIECE), jnp.int32),
            pltpu.VMEM((8, PIECE), F32),
            dma((2,)), dma((2,)), dma((7,)), dma((7,)), dma, dma((PARTS,)), dma, dma((PARTS,)), dma((7,)), dma((7,)), dma((2,)),
        ],
        compiler_params=pltpu.CompilerParams(
            collective_id=3, has_side_effects=True, vmem_limit_bytes=32 << 20
        ),
    )(lead, pieces, lead_logits, labels)


def per_device(
    tokens, norm_gain, w_query, w_key, w_value, w_out, w_up, w_class, starts, lengths, labels
):
    att, w_full, base = attend(tokens.T, norm_gain.reshape(D // HD, HD), w_query, w_key, w_value, w_out, w_up)
    expanded = expand(att, base, w_full, w_up)
    own, lead, logits, lead_logits = place(starts, lengths, expanded, w_class.T)
    arriving, loss = losses(lead, logits, lead_logits, labels.T)
    features = own.at[NUC - LEAD :].add(arriving)
    return (features, loss[:, 0, :].reshape(-1)[:NUC])


def solution(mesh):
    return jax.shard_map(
        per_device,
        mesh=mesh,
        in_specs=(
            P("seq", "mp"),
            P(),
            P(None, "mp"),
            P(None, "mp"),
            P(None, "mp"),
            P("mp", None),
            P(None, None, "mp"),
            P("mp", None),
            P("seq"),
            P("seq"),
            P("seq", None),
        ),
        out_specs=(P("seq", "mp"), P("seq")),
        check_vma=False,
    )
```
